128 devices in a mesh: row: 8 (over x, core), col: 16 (over z, y).
Axes of the slice: x: 4, y: 4, z: 4, core: 2. Of those that a mesh axis runs over, the one named last changes fastest.
Arguments:
- jac_cam: float32 [8, 18, 16384], P(None, None, ('row', 'col')), may hold values from -4 to 4
- jac_pt: float32 [8, 6, 16384], P(None, None, ('row', 'col')), may hold values from -6 to 6
- resid: float32 [8, 2, 16384], P(None, None, ('row', 'col')), may hold values from -6 to 6
- point_damp: float32 [3, 16384], P(None, ('row', 'col')), may hold values from 0.2 to 2
- cam_damp: float32 [16, 576], P('col'), may hold values from 0.5 to 4
- obs_cluster: int32 [16384, 8], P(('row', 'col')), may hold values from 0 to 15, all different within a row; in each aligned block of 128 rows (0 to 127, 128 to 255, ...) at most 96 rows name the same one
- obs_slot: int32 [8, 16384], P(None, ('row', 'col')), may hold values from 0 to 63
Outputs:
- schur: float32 [16, 16, 576, 576], P('row', 'col')
- step: float32 [9216], replicated
- residual: float32 [9216], replicated
- direction: float32 [9216], replicated
The draws below stay inside these ranges and needn't reach their ends.
Inputs may be any that keep to these rules, and one draw needn't show every extreme that they name: `obs_cluster`: the 8 observations of a point lie in 8 different clusters. Among the 128 points of one device (aligned blocks of rows), no cluster is named by more than 96 points, and in every draw some cluster is named by exactly 96 points of some device.
All inputs are finite; a program needn't handle non-finite values.
Results may differ from the reference program's by a relative error of at most 0.0003.
Values sent between devices are 32-bit elements; how exact they have to be, the bound alone decides.
No kernel may reach another device: no remote copies, remote signals or barrier semaphores. Data moves between devices by JAX's collectives and lax.ppermute only.
A program may use at most 192 MiB of HBM per device.

```python
import math
import jax
import jax.numpy as jnp
import numpy as np
from jax import lax

CAM = 64
TILE = 576
KOBS = 8
NPTS_DEV = 128
NCL = 16
CAP = 96
NPTS = 16384


def place_ends(drawn, rng, smallest, top_value):
    longest = drawn.shape.index(max(drawn.shape))
    spots = []
    for shift in (0, 1):
        where = [jax.random.randint(jax.random.fold_in(rng, axis), (), 0, length) for axis, length in enumerate(drawn.shape)]
        where[longest] = (where[longest] + shift) % drawn.shape[longest]
        spots.append(tuple(where))
    return drawn.at[spots[0]].set(smallest).at[spots[1]].set(top_value)


def shard_levels(key, dims, cuts, low, high):
    loudness = 1.0
    for axis_at, blocks in cuts:
        heights = jax.random.uniform(jax.random.fold_in(jax.random.fold_in(key, 6), axis_at), (blocks,), jnp.float32, low / len(cuts), high / len(cuts))
        loudness = loudness * jnp.repeat(jnp.exp(heights), dims[axis_at] // blocks).reshape((-1,) + (1,) * (len(dims) - 1 - axis_at))
    return loudness


def shared_out(own_key, own, number, rows, amount, top, limit, slope):
    sequence = jax.random.permutation(own_key, amount)
    heavy_load, usual = load_shares(amount, rows * top, limit, slope, True), load_shares(amount, rows * top, limit, slope, False)
    places = jnp.arange(amount)

    def named(lengths, offset_by):
        used = int((lengths > 0).sum())
        fixed = max(1, used // 4)
        passed = fixed + (places - fixed + offset_by * (used - fixed)) % max(1, amount - fixed)
        return jnp.zeros((amount,), jnp.int32).at[sequence[jnp.where(places < fixed, places, passed)]].set(jnp.asarray(lengths, jnp.int32))

    lengths = jnp.where(number % 4 == 0, named(heavy_load, number // 4), named(usual, number - number // 4 - 1))
    mixed = jax.random.permutation(jax.random.fold_in(own, 3), amount)
    source_of, sink = mixed[0:amount // 2 * 2:2], mixed[1:amount // 2 * 2:2]
    room = jnp.minimum(lengths[source_of] - 1, limit - lengths[sink]) // 2
    room = jnp.where((source_of == sequence[0]) | (sink == sequence[0]) | (lengths[sink] == 0), 0, jnp.maximum(room, 0))
    passed = jax.random.randint(jax.random.fold_in(own, 4), (amount // 2,), 0, 1 << 20) % (room + 1)
    lengths = lengths.at[source_of].add(-passed).at[sink].add(passed)
    items = jnp.searchsorted(jnp.cumsum(lengths), jnp.arange(rows * top), side="right").astype(jnp.int32)
    grid = items.reshape(top, rows).T
    grid = grid[jax.random.permutation(jax.random.fold_in(own, 1), rows)]
    offset_by = jax.random.randint(jax.random.fold_in(own, 2), (rows, 1), 0, top)
    return jnp.take_along_axis(grid, (jnp.arange(top)[None, :] + offset_by) % top, axis=1)


def load_shares(count, total, reach, skew, full):
    weights = [(1 << 20) // math.isqrt(grade ** skew) + 1 for grade in range(1, count + 1)]
    largest = reach if full else min(reach, max(-(-total // count), total * weights[0] // sum(weights)))
    least = 1 if total - largest >= count - 1 else 0
    holding, surplus = [largest] + [least] * (count - 1), total - largest - least * (count - 1)
    while surplus > 0:
        movable = [i for i in range(1, count) if holding[i] < largest] or [i for i in range(1, count) if holding[i] < reach]
        whole, remaining = sum([weights[i] for i in movable]), surplus
        for i in movable:
            extra = min(reach - holding[i], max(1, remaining * weights[i] // whole), surplus)
            holding[i] = holding[i] + extra
            surplus = surplus - extra
    return np.array(holding)


def centred(own_key, extent, width, bound, shards=(), dtype=jnp.bfloat16):
    drawn = jax.random.normal(own_key, extent, jnp.float32) * width
    if len(shards) > 0:
        drawn = shard_levels(own_key, extent, shards, -0.22, 0.18) * drawn
    return jnp.clip(drawn, min=-bound, max=bound).astype(dtype)


def setup_inputs(seed: int = 0) -> dict:
    key_of = jax.random.split(jax.random.key(seed), 8)
    jac_cam = centred(key_of[0], (KOBS, 18, NPTS), 0.25, 4.0, ((2, 128),), jnp.float32)
    jac_pt = centred(key_of[1], (KOBS, 6, NPTS), 1.0, 6.0, ((2, 128),), jnp.float32)
    resid = centred(key_of[2], (KOBS, 2, NPTS), 1.0, 6.0, ((2, 128),), jnp.float32)
    point_damp = jnp.clip(jnp.exp(math.log(2.0) - 2.3025851 * jax.random.uniform(key_of[3], (3, NPTS), jnp.float32) ** shard_levels(key_of[3], (3, NPTS), ((1, 128),), -0.2, 0.2)), 0.2, 2.0)
    cam_damp = jnp.clip(jnp.exp(math.log(4.0) - 2.0794415 * jax.random.uniform(key_of[4], (NCL, TILE), jnp.float32) ** shard_levels(key_of[4], (NCL, TILE), ((0, 16),), -0.2, 0.2)), 0.5, 4.0)
    obs_cluster_keys = jax.random.split(jax.random.fold_in(key_of[5], 1), NPTS // NPTS_DEV)
    obs_cluster_turns = jax.random.permutation(jax.random.fold_in(key_of[5], 3), NPTS // NPTS_DEV)
    obs_cluster = jax.vmap(lambda own, number: shared_out(jax.random.fold_in(key_of[5], 2), own, number, NPTS_DEV, NCL, KOBS, CAP, 2))(obs_cluster_keys, obs_cluster_turns).reshape((NPTS, KOBS))
    obs_slot = place_ends(jax.random.randint(key_of[6], (KOBS, NPTS), 0, CAM), jax.random.fold_in(key_of[6], 1), 0, CAM - 1).astype(jnp.int32)
    return dict(jac_cam=jac_cam, jac_pt=jac_pt, resid=resid, point_damp=point_damp, cam_damp=cam_damp, obs_cluster=obs_cluster, obs_slot=obs_slot)


def point_factors(jac_cam, jac_pt, resid, point_damp):
    cam_rows = jac_cam.reshape(KOBS, 2, 9, -1)
    pnt_rows = jac_pt.reshape(KOBS, 2, 3, -1)

    def inner(first, second):
        return lax.optimization_barrier(jnp.sum(pnt_rows[:, :, first, :] * pnt_rows[:, :, second, :], axis=(0, 1)))
    diag_aa = inner(0, 0) + point_damp[0]
    diag_bb = inner(1, 1) + point_damp[1]
    diag_cc = inner(2, 2) + point_damp[2]
    lower_aa = jnp.sqrt(diag_aa)
    lower_ba = inner(1, 0) / lower_aa
    lower_ca = inner(2, 0) / lower_aa
    lower_bb = jnp.sqrt(diag_bb - lower_ba * lower_ba)
    lower_cb = (inner(2, 1) - lower_ca * lower_ba) / lower_bb
    lower_cc = jnp.sqrt(diag_cc - lower_ca * lower_ca - lower_cb * lower_cb)

    def solve_lower(vec_a, vec_b, vec_c):
        out_a = vec_a / lower_aa
        out_b = (vec_b - lower_ba * out_a) / lower_bb
        out_c = (vec_c - lower_ca * out_a - lower_cb * out_b) / lower_cc
        return [out_a, out_b, out_c]
    whiten = solve_lower(pnt_rows[:, :, 0, :], pnt_rows[:, :, 1, :], pnt_rows[:, :, 2, :])
    coupled = [lax.optimization_barrier(jnp.sum(cam_rows * part[:, :, None, :], axis=1)) for part in whiten]
    grads = [lax.optimization_barrier(jnp.sum(pnt_rows[:, :, member, :] * resid, axis=(0, 1))) for member in range(3)]
    reduced = solve_lower(grads[0], grads[1], grads[2])
    factor = jnp.stack([cam_rows[:, 0], cam_rows[:, 1]] + coupled, axis=1)
    shaped = [jnp.broadcast_to(part, resid[:, 0].shape) for part in reduced]
    targets = jnp.stack([-resid[:, 0], -resid[:, 1]] + shaped, axis=1)
    return (factor, targets)

def reference(jac_cam, jac_pt, resid, point_damp, cam_damp, obs_cluster, obs_slot):
    factor, targets = point_factors(jac_cam, jac_pt, resid, point_damp)
    clusters = obs_cluster.T
    blocks = jnp.zeros((NCL, NCL, CAM * CAM, 81), jnp.float32)
    rhs = jnp.zeros((NCL * CAM, 9), jnp.float32)
    for first in range(KOBS):
        for second in range(KOBS):
            if first == second:
                signs = jnp.array([1.0, 1.0, -1.0, -1.0, -1.0], jnp.float32)
            else:
                signs = jnp.array([0.0, 0.0, -1.0, -1.0, -1.0], jnp.float32)
            product = lax.optimization_barrier(jnp.sum(factor[first][:, :, None, :] * signs[:, None, None, None] * factor[second][:, None, :, :], axis=0))
            where = obs_slot[first] * CAM + obs_slot[second]
            blocks = blocks.at[clusters[first], clusters[second], where].add(product.reshape(81, -1).T)
        term = lax.optimization_barrier(jnp.sum(factor[first] * targets[first][:, None, :], axis=0))
        rhs = rhs.at[clusters[first] * CAM + obs_slot[first]].add(term.T)
    schur = blocks.reshape(NCL, NCL, CAM, CAM, 9, 9).transpose(0, 1, 2, 4, 3, 5).reshape(NCL, NCL, TILE, TILE)
    serial = jnp.arange(NCL)
    schur = schur.at[serial, serial].add(jax.vmap(jnp.diag)(cam_damp))
    rhs = rhs.reshape(NCL * TILE)
    precond = jnp.diagonal(schur[serial, serial], axis1=1, axis2=2).reshape(NCL * TILE)
    matrix = schur.transpose(0, 2, 1, 3).reshape(NCL * TILE, NCL * TILE)
    start = rhs / precond
    rz_first = jnp.sum(rhs * start)
    image = jnp.dot(matrix, start, precision=lax.Precision.HIGHEST)
    alpha = rz_first / jnp.sum(start * image)
    step = alpha * start
    residual = rhs - alpha * image
    second_z = residual / precond
    beta = jnp.sum(residual * second_z) / rz_first
    direction = second_z + beta * start
    return (schur, step, residual, direction)
```

```python
import functools

import jax
import jax.numpy as jnp
from jax import lax
from jax.experimental import pallas as pl
from jax.experimental.pallas import tpu as pltpu
from jax.sharding import PartitionSpec as P

KOBS = 8
NCL = 16
CAP = 96
CAM = 64
TILE = 576
NROW = 8
NDEV = 128
PTS = 128
AXES = ("row", "col")
BF = jnp.bfloat16
F32 = jnp.float32
NT = (((1,), (1,)), ((), ()))
MIB = 1 << 20


def iota(shape, dim):
    return lax.broadcasted_iota(jnp.int32, shape, dim)


def whitened(jp, rs, damp):
    def inner(a, b):
        return jnp.sum(jp[0][a] * jp[0][b] + jp[1][a] * jp[1][b], axis=0, keepdims=True)

    laa = jnp.sqrt(inner(0, 0) + damp[0:1])
    lba = inner(1, 0) / laa
    lca = inner(2, 0) / laa
    lbb = jnp.sqrt(inner(1, 1) + damp[1:2] - lba * lba)
    lcb = (inner(2, 1) - lca * lba) / lbb
    lcc = jnp.sqrt(inner(2, 2) + damp[2:3] - lca * lca - lcb * lcb)

    def solve(a, b, c):
        x = a / laa
        y = (b - lba * x) / lbb
        return [x, y, (c - lca * x - lcb * y) / lcc]

    u = [solve(*jp[m]) for m in range(2)]
    grad = [
        jnp.sum(jp[0][a] * rs[0] + jp[1][a] * rs[1], axis=0, keepdims=True) for a in range(3)
    ]
    w = solve(*grad)
    q = [u[m][0] * w[0] + u[m][1] * w[1] + u[m][2] * w[2] - rs[m] for m in range(2)]
    return u, q


def load_point(jp_ref, rs_ref, damp_ref):
    jp = [[jp_ref[m * 3 + a] for a in range(3)] for m in range(2)]
    rs = [rs_ref[m] for m in range(2)]
    return whitened(jp, rs, damp_ref[...])


def pack_kernel(jc_ref, jp_ref, rs_ref, damp_ref, cl_ref, slot_ref, out_ref, fields, dense):
    u, _ = load_point(jp_ref, rs_ref, damp_ref)
    j0, j1 = jc_ref[0], jc_ref[9]
    top = jnp.maximum(jnp.abs(j0), jnp.abs(j1))
    some = top > 0.0
    safe = jnp.where(some, top, 1.0)
    x, y = j0 / safe, j1 / safe
    length = jnp.where(some, jnp.sqrt(x * x + y * y), 1.0)
    cs = jnp.where(some, x / length, 1.0)
    sn = jnp.where(some, y / length, 0.0)
    for i in range(9):
        a, b = jc_ref[i], jc_ref[9 + i]
        fields[i] = cs * a + sn * b
        if i:
            fields[8 + i] = cs * b - sn * a
    for a in range(3):
        fields[17 + a] = cs * u[0][a] + sn * u[1][a]
        fields[20 + a] = cs * u[1][a] - sn * u[0][a]
    fields[23] = slot_ref[...].astype(F32)
    named = []
    for e in range(2):
        ids = 2 * iota((NROW, PTS), 0) + e
        hits = [jnp.broadcast_to(cl_ref[k : k + 1, :], (NROW, PTS)) == ids for k in range(KOBS)]
        for f in range(24):
            value = jnp.full((NROW, PTS), -1.0 if f == 23 else 0.0, F32)
            for k in range(KOBS):
                row = jnp.broadcast_to(fields[f, k : k + 1, :], (NROW, PTS))
                value = jnp.where(hits[k], row, value)
            dense[f, e] = value
        named.append(dense[23, e] >= 0.0)
    present = jnp.concatenate([n.astype(F32) for n in named], axis=0).astype(BF)
    upto = (iota((PTS, PTS), 1) <= iota((PTS, PTS), 0)).astype(F32).astype(BF)
    counts = lax.dot_general(upto, present, NT, preferred_element_type=F32)
    lane = iota((NROW, PTS), 1)
    lane_f = iota((PTS, PTS), 1).astype(F32)
    ones = jnp.ones((NROW, PTS), BF)
    row_id = iota((NROW, PTS), 0)
    for c in range(NCL):
        ec, rc = c % 2, c // 2
        col = ec * NROW + rc
        before = (jnp.broadcast_to(counts[:, col : col + 1], (PTS, PTS)) <= lane_f).astype(F32)
        found = jnp.dot(ones, before.astype(BF), preferred_element_type=F32)
        valid = found < float(PTS)
        pick = jnp.minimum(found, float(PTS - 1)).astype(jnp.int32)

        def take(f, e):
            return jnp.take_along_axis(dense[f, e], pick, axis=1)

        side = [[take(f, e) for f in range(24)] for e in range(2)]
        mine = [jnp.broadcast_to(side[ec][f][rc : rc + 1, :], (NROW, PTS)) for f in range(24)]
        mid = []
        for e in range(2):
            on = jnp.where(2 * row_id + e == c, 1.0, 0.0)
            for m in range(2):
                for n in range(2):
                    v = sum(side[e][17 + 3 * m + a] * mine[17 + 3 * n + a] for a in range(3))
                    mid.append(on - v if m == n else -v)
        rows = []
        for part in (side[0], side[1], mine):
            rows += part[0:9] + part[9:16]
        extra = [side[0][16], side[1][16], mine[16], side[0][23], side[1][23]]
        extra.append(jnp.where(valid, mine[23], -1.0))
        zero = jnp.zeros((NROW, PTS), F32)
        extra += [zero, zero] + mid
        for v in range(3):
            for q in range(16):
                moved = extra[q] if q in (6, 7) else pltpu.roll(extra[q], 96 - 32 * v, 1)
                full = jnp.where(lane < CAP, rows[v * 16 + q], moved)
                out_ref[:, c, v * 16 + q, :] = full


def pack(jc, jp, rs, damp, cl, slot):
    return pl.pallas_call(
        pack_kernel,
        out_shape=jax.ShapeDtypeStruct((NROW, NCL, 48, PTS), F32),
        scratch_shapes=[
            pltpu.VMEM((24, KOBS, PTS), F32),
            pltpu.VMEM((24, 2, NROW, PTS), F32),
        ],
        compiler_params=pltpu.CompilerParams(vmem_limit_bytes=40 * MIB),
        cost_estimate=pl.CostEstimate(flops=10**7, bytes_accessed=4 * 10**6, transcendentals=0),
        name="pack",
    )(jc, jp, rs, damp, cl, slot)


SRC = 8
LANES = SRC * CAP
GROUP = 3


def spread_kernel(flag_ref, in_ref, damp_ref, out_ref, acc, rows_ref, prod, stage):
    step = pl.program_id(0)

    @pl.when(step == 0)
    def _():
        acc[...] = jnp.zeros_like(acc)

    for half in range(SRC // 4):
        pieces = []
        for s in range(4):
            block = in_ref[half * 4 + s]
            lane16 = iota((16, PTS), 1)
            rest = jnp.where(
                lane16 < 32,
                pltpu.roll(block[0:16], 32, 1),
                jnp.where(lane16 < 64, pltpu.roll(block[16:32], 64, 1), pltpu.roll(block[32:48], 96, 1)),
            )
            pieces.append(jnp.concatenate([block, rest], axis=0))
        lane = iota((64, PTS), 1)
        r1, r2, r3 = pltpu.roll(pieces[1], 96, 1), pltpu.roll(pieces[2], 64, 1), pltpu.roll(pieces[3], 32, 1)
        base = half * 384
        rows_ref[:, base : base + 128] = jnp.where(lane < 96, pieces[0], r1)
        rows_ref[:, base + 128 : base + 256] = jnp.where(lane < 64, r1, r2)
        rows_ref[:, base + 256 : base + 384] = jnp.where(lane < 32, r2, r3)

    def bcast(row, n):
        return jnp.broadcast_to(row, (n, LANES))

    first = iota((8, LANES), 0) == 0
    cam0 = rows_ref[32:40]
    cam1 = jnp.where(first, 0.0, rows_ref[40:48])
    slot_c = rows_ref[53:54].astype(jnp.int32)
    for e in range(2):
        a0 = rows_ref[16 * e : 16 * e + 8]
        a1 = jnp.where(first, 0.0, rows_ref[16 * e + 8 : 16 * e + 16])
        last0 = rows_ref[16 * e + 8 : 16 * e + 9]
        last1 = rows_ref[48 + e : 49 + e]
        t, t_last = [], []
        for m in range(2):
            m0 = rows_ref[56 + 4 * e + 2 * m : 57 + 4 * e + 2 * m]
            m1 = rows_ref[57 + 4 * e + 2 * m : 58 + 4 * e + 2 * m]
            t.append(bcast(m0, 8) * cam0 + bcast(m1, 8) * cam1)
            t_last.append(m0 * rows_ref[40:41] + m1 * rows_ref[50:51])

        def split(value):
            high = value.astype(BF).astype(F32)
            return high, value - high

        for j in range(9):
            t0 = t[0][j : j + 1] if j < 8 else t_last[0]
            t1 = t[1][j : j + 1] if j < 8 else t_last[1]
            high, low = split(a0 * bcast(t0, 8) + a1 * bcast(t1, 8))
            prod[0, j, 0:8] = high
            prod[1, j, 0:8] = low
            high, low = split(last0 * t0 + last1 * t1)
            prod[0, j, 8:9] = high
            prod[1, j, 8:9] = low

        slot_a = rows_ref[51 + e : 52 + e].astype(jnp.int32)
        both = jnp.minimum(slot_a, slot_c) >= 0
        code = jnp.where(both, (slot_a >> 4) * CAM + slot_c, -1)
        onehot = (bcast(code, 256) == iota((256, LANES), 0)).astype(F32).astype(BF)
        mask = (bcast(slot_a & 15, 16) == iota((16, LANES), 0)).astype(F32).astype(BF)
        for g in range(9 // GROUP):
            parts = []
            for h in range(2):
                for j in range(g * GROUP, (g + 1) * GROUP):
                    for i in range(9):
                        parts.append(bcast(prod[h, j, i : i + 1], 16).astype(BF) * mask)
            left = jnp.concatenate(parts, axis=0)
            got = lax.dot_general(left, onehot, NT, preferred_element_type=F32)
            n = GROUP * 144
            acc[e, g * n : (g + 1) * n, :] += got[:n] + got[n:]

    @pl.when(step == pl.num_programs(0) - 1)
    def _():
        source = iota((640, 640), 0)
        place = iota((640, 640), 1) == 9 * (source % CAM) + source // CAM
        place = (place & (source < TILE)).astype(F32).astype(BF)
        lane = iota((144, PTS), 1)
        for e in range(2):
            for u in range(4):
                base = (u // 2) * 128
                tiles = []
                for jj in range(5):
                    even = acc[e, 288 * jj : 288 * jj + 144, base : base + 128]
                    if u % 2:
                        even = pltpu.roll(even, 64, 1)
                    if jj < 4:
                        odd = acc[e, 288 * jj + 144 : 288 * jj + 288, base : base + 128]
                        if u % 2 == 0:
                            odd = pltpu.roll(odd, 64, 1)
                        even = jnp.where(lane < CAM, even, odd)
                    tiles.append(even)
                wide = jnp.concatenate(tiles, axis=1)
                high = wide.astype(BF)
                low = (wide - high.astype(F32)).astype(BF)
                got = jnp.dot(high, place, preferred_element_type=F32)
                got += jnp.dot(low, place, preferred_element_type=F32)
                for tile in range(5):
                    for i in range(9):
                        piece = got[16 * i : 16 * i + 16, 128 * tile : 128 * tile + 128]
                        stage[pl.ds(TILE * tile + 144 * u + i, 16, stride=9), :] = piece
            for tile in range(5):
                wide = min(128, TILE - 128 * tile)
                block = stage[TILE * tile : TILE * tile + TILE, 0:wide]
                out_ref[e, :, 128 * tile : 128 * tile + wide] = block

            @pl.when(flag_ref[e] == 1)
            def _():
                same = iota((TILE, TILE), 0) == iota((TILE, TILE), 1)
                out_ref[e] += jnp.where(same, jnp.broadcast_to(damp_ref[...], (TILE, TILE)), 0.0)


def spread(flags, incoming, damp):
    steps = NDEV // SRC
    return pl.pallas_call(
        spread_kernel,
        grid=(steps,),
        in_specs=[
            pl.BlockSpec(memory_space=pltpu.SMEM),
            pl.BlockSpec((SRC, 48, PTS), lambda s: (s, 0, 0)),
            pl.BlockSpec((1, TILE), lambda s: (0, 0)),
        ],
        out_specs=pl.BlockSpec((2, TILE, TILE), lambda s: (0, 0, 0)),
        out_shape=jax.ShapeDtypeStruct((2, TILE, TILE), F32),
        scratch_shapes=[
            pltpu.VMEM((2, 1296, 256), F32),
            pltpu.VMEM((64, LANES), F32),
            pltpu.VMEM((2, 9, 16, LANES), F32),
            pltpu.VMEM((5 * TILE, 128), F32),
        ],
        compiler_params=pltpu.CompilerParams(vmem_limit_bytes=48 * MIB),
        cost_estimate=pl.CostEstimate(flops=4 * 10**10, bytes_accessed=6 * 10**6, transcendentals=0),
        name="spread",
    )(flags, incoming, damp)


def three(value):
    a = value.astype(BF)
    rest = value - a.astype(F32)
    b = rest.astype(BF)
    c = (rest - b.astype(F32)).astype(BF)
    return jnp.concatenate([a, b, c], axis=0)


NCAM = NCL * CAM


def camera_hits(cl_ref, slot_ref, k):
    code = cl_ref[k : k + 1, :] * CAM + slot_ref[k : k + 1, :]
    hit = jnp.broadcast_to(code, (NCAM, PTS)) == iota((NCAM, PTS), 0)
    return hit.astype(F32).astype(BF)


def sums_kernel(jc_ref, jp_ref, rs_ref, damp_ref, cl_ref, slot_ref, out_ref):
    u, q = load_point(jp_ref, rs_ref, damp_ref)
    m00 = 1.0 - (u[0][0] * u[0][0] + u[0][1] * u[0][1] + u[0][2] * u[0][2])
    m11 = 1.0 - (u[1][0] * u[1][0] + u[1][1] * u[1][1] + u[1][2] * u[1][2])
    m01 = -2.0 * (u[0][0] * u[1][0] + u[0][1] * u[1][1] + u[0][2] * u[1][2])
    terms = []
    for i in range(9):
        a, b = jc_ref[i], jc_ref[9 + i]
        terms.append(a * q[0] + b * q[1])
    for i in range(9):
        a, b = jc_ref[i], jc_ref[9 + i]
        terms.append(a * a * m00 + a * b * m01 + b * b * m11)
    total = jnp.zeros((72, NCAM), F32)
    pad = jnp.zeros((6, PTS), F32)
    for k in range(KOBS):
        stacked = jnp.concatenate([v[k : k + 1] for v in terms] + [pad], axis=0)
        total += lax.dot_general(
            three(stacked), camera_hits(cl_ref, slot_ref, k), NT, preferred_element_type=F32
        )
    out_ref[...] = (total[0:24] + total[24:48] + total[48:72])[0:18]


def image_kernel(first_ref, jc_ref, jp_ref, rs_ref, damp_ref, cl_ref, slot_ref, out_ref):
    u, _ = load_point(jp_ref, rs_ref, damp_ref)
    pad = jnp.zeros((7, NCAM), F32)
    first = three(jnp.concatenate([first_ref[...], pad], axis=0))
    hits = [camera_hits(cl_ref, slot_ref, k) for k in range(KOBS)]
    seen = [[], []]
    for k in range(KOBS):
        got = jnp.dot(first, hits[k], preferred_element_type=F32)
        x = got[0:16] + got[16:32] + got[32:48]
        for m in range(2):
            row = sum(jc_ref[9 * m + i][k : k + 1] * x[i : i + 1] for i in range(9))
            seen[m].append(row)
    y = [jnp.concatenate(rows, axis=0) for rows in seen]
    z = [jnp.sum(u[0][a] * y[0] + u[1][a] * y[1], axis=0, keepdims=True) for a in range(3)]
    v = [y[m] - (u[m][0] * z[0] + u[m][1] * z[1] + u[m][2] * z[2]) for m in range(2)]
    terms = [jc_ref[i] * v[0] + jc_ref[9 + i] * v[1] for i in range(9)]
    total = jnp.zeros((48, NCAM), F32)
    pad = jnp.zeros((7, PTS), F32)
    for k in range(KOBS):
        stacked = jnp.concatenate([t[k : k + 1] for t in terms] + [pad], axis=0)
        total += lax.dot_general(three(stacked), hits[k], NT, preferred_element_type=F32)
    out_ref[...] = (total[0:16] + total[16:32] + total[32:48])[0:9]


def small_call(body, rows, name, *args):
    return pl.pallas_call(
        body,
        out_shape=jax.ShapeDtypeStruct((rows, NCAM), F32),
        compiler_params=pltpu.CompilerParams(vmem_limit_bytes=32 * MIB),
        cost_estimate=pl.CostEstimate(flops=3 * 10**8, bytes_accessed=10**6, transcendentals=0),
        name=name,
    )(*args)


def finish_kernel(rhs_ref, diag_ref, image_ref, step_ref, res_ref, dir_ref):
    rhs, diag, image = rhs_ref[...], diag_ref[...], image_ref[...]
    start = rhs / diag
    rz = jnp.sum(rhs * start)
    alpha = rz / jnp.sum(start * image)
    residual = rhs - alpha * image
    second = residual / diag
    beta = jnp.sum(residual * second) / rz
    step_ref[...] = alpha * start
    res_ref[...] = residual
    dir_ref[...] = second + beta * start


def total_sum(value):
    shape = value.shape
    flat = value.reshape(-1, 128)
    for bit in (16, 32, 64, 1, 2, 4, 8):
        pairs = [(d, d ^ bit) for d in range(NDEV)]
        flat = flat + lax.ppermute(flat, AXES, pairs)
    return flat.reshape(shape)


def shards(jac_cam, jac_pt, resid, point_damp, cam_damp, obs_cluster, obs_slot):
    my_row = lax.axis_index("row")
    my_col = lax.axis_index("col")
    jc = jac_cam.transpose(1, 0, 2)
    jp = jac_pt.transpose(1, 0, 2)
    rs = resid.transpose(1, 0, 2)
    cl = obs_cluster.T
    packed = pack(jc, jp, rs, point_damp, cl, obs_slot)
    incoming = lax.all_to_all(
        packed.reshape(NDEV, 48, PTS), AXES, split_axis=0, concat_axis=0, tiled=True
    )
    here = (jnp.arange(NCL) == my_col) & (my_row == 0)
    damp = cam_damp.reshape(CAM, 9).T
    damp = (damp[:, None, :] * here.astype(F32)[None, :, None]).reshape(9, NCAM)

    sums = small_call(sums_kernel, 18, "sums", jc, jp, rs, point_damp, cl, obs_slot)
    sums = total_sum(sums + jnp.concatenate([jnp.zeros_like(damp), damp], axis=0))
    rhs, diag = sums[0:9], sums[9:18]
    first = rhs / diag
    image = small_call(
        image_kernel, 9, "image", first, jc, jp, rs, point_damp, cl, obs_slot
    )
    image = total_sum(image + damp * first)
    step, residual, direction = pl.pallas_call(
        finish_kernel,
        out_shape=[jax.ShapeDtypeStruct((9, NCAM), F32)] * 3,
        name="finish",
    )(rhs, diag, image)
    flags = (2 * my_row + jnp.arange(2) == my_col).astype(jnp.int32)
    schur = spread(flags, incoming, cam_damp)

    def order(value):
        return value.T.reshape(-1)

    return (schur[:, None], order(step), order(residual), order(direction))


def solution(mesh):
    placed = (
        P(None, None, AXES),
        P(None, None, AXES),
        P(None, None, AXES),
        P(None, AXES),
        P("col", None),
        P(AXES, None),
        P(None, AXES),
    )
    return jax.shard_map(
        shards,
        mesh=mesh,
        in_specs=placed,
        out_specs=(P("row", "col", None, None), P(), P(), P()),
        check_vma=False,
    )
```

```python
import functools

import jax
import jax.numpy as jnp
from jax import lax
from jax.experimental import pallas as pl
from jax.experimental.pallas import tpu as pltpu
from jax.sharding import PartitionSpec as P

KOBS = 8
NCL = 16
CAP = 96
CAM = 64
TILE = 576
NROW = 8
NDEV = 128
PTS = 128
AXES = ("row", "col")
BF = jnp.bfloat16
F32 = jnp.float32
NT = (((1,), (1,)), ((), ()))
MIB = 1 << 20
SRC = 16
LANES = SRC * CAP
GROUP = 3
ANY = pl.BlockSpec(memory_space=pl.ANY)


def iota(shape, dim):
    return lax.broadcasted_iota(jnp.int32, shape, dim)


def whole(*shape):
    return pl.BlockSpec(shape, lambda *_: (0,) * len(shape))


def settings(micros, mib):
    return dict(
        compiler_params=pltpu.CompilerParams(vmem_limit_bytes=mib * MIB),
        cost_estimate=pl.CostEstimate(
            flops=micros * 10**9, bytes_accessed=10**6, transcendentals=0
        ),
    )


def lanes_of(row, n):
    return jnp.broadcast_to(row, (n, row.shape[1]))


def whitened(jp, rs, damp):
    def inner(a, b):
        return jnp.sum(jp[0][a] * jp[0][b] + jp[1][a] * jp[1][b], axis=0, keepdims=True)

    laa = jnp.sqrt(inner(0, 0) + damp[0:1])
    lba = inner(1, 0) / laa
    lca = inner(2, 0) / laa
    lbb = jnp.sqrt(inner(1, 1) + damp[1:2] - lba * lba)
    lcb = (inner(2, 1) - lca * lba) / lbb
    lcc = jnp.sqrt(inner(2, 2) + damp[2:3] - lca * lca - lcb * lcb)

    def solve(a, b, c):
        x = a / laa
        y = (b - lba * x) / lbb
        return [x, y, (c - lca * x - lcb * y) / lcc]

    u = [solve(*jp[m]) for m in range(2)]
    grad = [
        jnp.sum(jp[0][a] * rs[0] + jp[1][a] * rs[1], axis=0, keepdims=True) for a in range(3)
    ]
    w = solve(*grad)
    q = [u[m][0] * w[0] + u[m][1] * w[1] + u[m][2] * w[2] - rs[m] for m in range(2)]
    return u, q


def three(value):
    a = value.astype(BF)
    rest = value - a.astype(F32)
    b = rest.astype(BF)
    return jnp.concatenate([a, b, (rest - b.astype(F32)).astype(BF)], axis=0)


def chosen(dense, pair, ec):
    upto = (iota((PTS, PTS), 1) <= iota((PTS, PTS), 0)).astype(F32).astype(BF)
    lane = iota((PTS, PTS), 1).astype(F32)
    present = (dense[23, ec, pl.ds(pair, 1), :] >= 0.0).astype(F32)
    present = lanes_of(present, PTS).astype(BF)
    counts = lax.dot_general(upto, present, NT, preferred_element_type=F32)
    before = (counts <= lane).astype(F32).astype(BF)
    return jnp.dot(jnp.ones((NROW, PTS), BF), before, preferred_element_type=F32)


def points_kernel(jc, jp, rs, damp, cl_ref, slot_ref, dense, found_ref, fields):
    cl, slot = cl_ref[...], slot_ref[...]
    u, q = whitened(
        [[jp[m * 3 + a] for a in range(3)] for m in range(2)],
        [rs[:, m, :] for m in range(2)],
        damp[...],
    )
    j0, j1 = jc[0], jc[9]
    top = jnp.maximum(jnp.abs(j0), jnp.abs(j1))
    some = top > 0.0
    safe = jnp.where(some, top, 1.0)
    x, y = j0 / safe, j1 / safe
    length = jnp.where(some, jnp.sqrt(x * x + y * y), 1.0)
    cs = jnp.where(some, x / length, 1.0)
    sn = jnp.where(some, y / length, 0.0)
    for i in range(9):
        a, b = jc[i], jc[9 + i]
        fields[i] = cs * a + sn * b
        if i:
            fields[8 + i] = cs * b - sn * a
    turned = [[], []]
    for a in range(3):
        turned[0].append(cs * u[0][a] + sn * u[1][a])
        turned[1].append(cs * u[1][a] - sn * u[0][a])
        fields[17 + a] = turned[0][a]
        fields[20 + a] = turned[1][a]
    fields[23] = slot.astype(F32)
    fields[24] = cs * q[0] + sn * q[1]
    fields[25] = cs * q[1] - sn * q[0]
    fields[26] = 1.0 - sum(v * v for v in turned[0])
    fields[27] = -2.0 * sum(v * w for v, w in zip(*turned))
    fields[28] = 1.0 - sum(v * v for v in turned[1])
    for e in range(2):
        ids = 2 * iota((NROW, PTS), 0) + e
        hits = [lanes_of(cl[k : k + 1], NROW) == ids for k in range(KOBS)]
        for f in range(29):
            value = jnp.full((NROW, PTS), -1.0 if f == 23 else 0.0, F32)
            for k in range(KOBS):
                value = jnp.where(hits[k], lanes_of(fields[f, k : k + 1, :], NROW), value)
            dense[f, e] = value
    for r in range(NROW):
        for e in range(2):
            found_ref[2 * r + e] = chosen(dense, r, e)


def points(*args):
    shapes = [(29, 2, NROW, PTS), (NCL, NROW, PTS)]
    return pl.pallas_call(
        points_kernel,
        grid=(1,),
        in_specs=[whole(*a.shape) for a in args],
        out_specs=[whole(*shape) for shape in shapes],
        out_shape=[jax.ShapeDtypeStruct(shape, F32) for shape in shapes],
        scratch_shapes=[pltpu.VMEM((29, KOBS, PTS), F32)],
        name="points",
        **settings(4, 60),
    )(*args)


def mixed(side, mine, on):
    out = []
    for m in range(2):
        for n in range(2):
            v = sum(side[17 + 3 * m + a] * mine[17 + 3 * n + a] for a in range(3))
            out.append(on - v if m == n else -v)
    return out


def pack_kernel(dense, found_ref, out_ref, kept):
    pair = pl.program_id(0)
    lane = iota((NROW, PTS), 1)
    zero = jnp.zeros((NROW, PTS), F32)
    for ec in range(2):
        found = found_ref[2 * pair + ec]
        pick = jnp.minimum(found, float(PTS - 1)).astype(jnp.int32)
        side = [
            [jnp.take_along_axis(dense[f, e], pick, axis=1) for f in range(24)] for e in range(2)
        ]
        for f in range(29):
            if f < 24:
                kept[f] = side[ec][f]
            else:
                kept[f] = jnp.take_along_axis(dense[f, ec], pick, axis=1)
        mine = [lanes_of(kept[f, pl.ds(pair, 1), :], NROW) for f in range(29)]
        rows = side[0][0:16] + side[1][0:16] + mine[0:16]
        rows += [side[0][16], side[1][16], mine[16], side[0][23], side[1][23]]
        rows.append(jnp.where(found < float(PTS), mine[23], -1.0))
        rows += mine[24:26]
        extra = []
        for e in range(2):
            same = jnp.where(iota((NROW, PTS), 0) == pair, float(e == ec), 0.0)
            extra += mixed(side[e], mine, same)
        extra += mine[26:29]
        for at, row in enumerate(rows):
            v, x = at // 16, at % 16
            rest = pltpu.roll(extra[x], 96 - 32 * v, 1) if v < 3 and x < 11 else zero
            out_ref[:, ec, at, :] = jnp.where(lane < CAP, row, rest)


def pack(dense, found):
    return pl.pallas_call(
        pack_kernel,
        grid=(NROW,),
        in_specs=[whole(29, 2, NROW, PTS), whole(NCL, NROW, PTS)],
        out_specs=pl.BlockSpec((NROW, 2, SENT, PTS), lambda g: (0, g, 0, 0)),
        out_shape=jax.ShapeDtypeStruct((NROW, NCL, SENT, PTS), F32),
        scratch_shapes=[pltpu.VMEM((29, NROW, PTS), F32)],
        name="pack",
        **settings(8, 60),
    )(dense, found)


def exchange(value):
    return lax.all_to_all(value, AXES, split_axis=0, concat_axis=0, tiled=True)


ROWS = 72
SENT = 56


def lay(in_ref, rows_ref):
    lane = iota((16, PTS), 1)
    full = iota((ROWS, PTS), 1)
    for quarter in range(SRC // 4):
        pieces = []
        for s in range(4):
            block = in_ref[quarter * 4 + s]
            part = [pltpu.roll(block[16 * v : 16 * v + 16], 32 + 32 * v, 1) for v in range(3)]
            rest = jnp.where(lane < 32, part[0], jnp.where(lane < 64, part[1], part[2]))
            pieces.append(jnp.concatenate([block, rest], axis=0))
        r1, r2 = pltpu.roll(pieces[1], 96, 1), pltpu.roll(pieces[2], 64, 1)
        r3 = pltpu.roll(pieces[3], 32, 1)
        base = quarter * 384
        rows_ref[:, base : base + 128] = jnp.where(full < 96, pieces[0], r1)
        rows_ref[:, base + 128 : base + 256] = jnp.where(full < 64, r1, r2)
        rows_ref[:, base + 256 : base + 384] = jnp.where(full < 32, r2, r3)


def jacobian(rows_ref, which):
    at = 16 * which
    first = iota((8, LANES), 0) == 0
    a1 = jnp.where(first, 0.0, rows_ref[at + 8 : at + 16])
    return rows_ref[at : at + 8], a1, rows_ref[at + 8 : at + 9], rows_ref[48 + which : 49 + which]


def cg_kernel(flag_ref, in_ref, damp_ref, rows_ref, out_ref, keep, hits, sums, image):
    step = pl.program_id(0)
    steps = pl.num_programs(0)

    @pl.when(step == 0)
    def _():
        sums[...] = jnp.zeros_like(sums)

    lay(in_ref, rows_ref)
    a0, a1, l0, l1 = jacobian(rows_ref, 2)
    q0, q1 = rows_ref[54:55], rows_ref[55:56]
    m0, m1, m2 = rows_ref[64:65], rows_ref[65:66], rows_ref[66:67]
    terms = [
        a0 * lanes_of(q0, 8) + a1 * lanes_of(q1, 8),
        a0 * a0 * lanes_of(m0, 8) + a0 * a1 * lanes_of(m1, 8) + a1 * a1 * lanes_of(m2, 8),
        l0 * q0 + l1 * q1,
        l0 * l0 * m0 + l0 * l1 * m1 + l1 * l1 * m2,
        jnp.zeros((6, LANES), F32),
    ]
    slot = rows_ref[53:54].astype(jnp.int32)
    hit = (lanes_of(slot, 128) == iota((128, LANES), 0)).astype(F32).astype(BF)
    hits[step] = hit
    keep[step] = rows_ref[...]
    sums[...] += lax.dot_general(
        three(jnp.concatenate(terms, axis=0)), hit, NT, preferred_element_type=F32
    )

    @pl.when(step == steps - 1)
    def _():
        damp = damp_ref[...]
        total = sums[0:24] + sums[24:48] + sums[48:72] + damp
        sums[0:24] = total
        x8, x9 = total[0:8] / total[8:16], total[16:17] / total[17:18]
        x = three(jnp.concatenate([x8, x9, jnp.zeros((7, 128), F32)], axis=0))
        image[...] = jnp.zeros_like(image)

        @pl.loop(0, steps)
        def _(at):
            rows = keep.at[at]
            got = jnp.dot(x, hits[at], preferred_element_type=F32)
            got = got[0:16] + got[16:32] + got[32:48]
            a0, a1, l0, l1 = jacobian(rows, 2)
            v0 = jnp.sum(a0 * got[0:8], axis=0, keepdims=True) + l0 * got[8:9]
            v1 = jnp.sum(a1 * got[0:8], axis=0, keepdims=True) + l1 * got[8:9]
            for e in range(2):
                m = [rows[56 + 4 * e + n : 57 + 4 * e + n] for n in range(4)]
                z0, z1 = m[0] * v0 + m[1] * v1, m[2] * v0 + m[3] * v1
                a0, a1, l0, l1 = jacobian(rows, e)
                out8 = a0 * lanes_of(z0, 8) + a1 * lanes_of(z1, 8)
                terms = [out8, l0 * z0 + l1 * z1, jnp.zeros((7, LANES), F32)]
                slot = rows[51 + e : 52 + e].astype(jnp.int32)
                slot = jnp.where(slot >= 0, slot + CAM * e, -1)
                hit = (lanes_of(slot, 128) == iota((128, LANES), 0)).astype(F32).astype(BF)
                image[...] += lax.dot_general(
                    three(jnp.concatenate(terms, axis=0)), hit, NT, preferred_element_type=F32
                )

        y = image[0:16] + image[16:32] + image[32:48]
        own = iota((16, 128), 1) < CAM
        extra = jnp.concatenate([damp[8:16] * x8, damp[17:18] * x9, jnp.zeros((7, 128), F32)], axis=0)
        extra = jnp.where(own, extra, 0.0)
        y += jnp.where(flag_ref[0] == 1, extra, 0.0)
        y += jnp.where(flag_ref[1] == 1, pltpu.roll(extra, CAM, 1), 0.0)
        part = sums[pl.ds(3 * flag_ref[2], 3), :]
        block = jnp.concatenate([y[0:9], part, jnp.zeros((4, 128), F32)], axis=0)
        out_ref[...] = jnp.broadcast_to(block[None], (NDEV, 16, 128))


def cg_part(flags, incoming, damp):
    steps = NDEV // SRC
    return pl.pallas_call(
        cg_kernel,
        grid=(steps,),
        in_specs=[
            pl.BlockSpec(memory_space=pltpu.SMEM),
            pl.BlockSpec((SRC, SENT, PTS), lambda s: (s, 0, 0)),
            whole(24, 128),
        ],
        out_specs=[pl.BlockSpec((ROWS, LANES), lambda s: (0, s)), whole(NDEV, 16, 128)],
        out_shape=[
            jax.ShapeDtypeStruct((ROWS, steps * LANES), F32),
            jax.ShapeDtypeStruct((NDEV, 16, 128), F32),
        ],
        scratch_shapes=[
            pltpu.VMEM((steps, ROWS, LANES), F32),
            pltpu.VMEM((steps, 128, LANES), BF),
            pltpu.VMEM((72, 128), F32),
            pltpu.VMEM((48, 128), F32),
        ],
        name="cg",
        **settings(6, 60),
    )(flags, incoming, damp)


def split(value):
    high = value.astype(BF).astype(F32)
    return high, value - high


def add_products(e, rows_ref, prod, acc):
    a0, a1, last0, last1 = jacobian(rows_ref, e)
    cam0, cam1, cam_last0, cam_last1 = jacobian(rows_ref, 2)
    t, t_last = [], []
    for m in range(2):
        at = 56 + 4 * e + 2 * m
        m0, m1 = rows_ref[at : at + 1], rows_ref[at + 1 : at + 2]
        t.append(lanes_of(m0, 8) * cam0 + lanes_of(m1, 8) * cam1)
        t_last.append(m0 * cam_last0 + m1 * cam_last1)
    for j in range(9):
        t0 = t[0][j : j + 1] if j < 8 else t_last[0]
        t1 = t[1][j : j + 1] if j < 8 else t_last[1]
        high, low = split(a0 * lanes_of(t0, 8) + a1 * lanes_of(t1, 8))
        prod[0, j, 0:8] = high
        prod[1, j, 0:8] = low
        high, low = split(last0 * t0 + last1 * t1)
        prod[0, j, 8:9] = high
        prod[1, j, 8:9] = low
    slot_a = rows_ref[51 + e : 52 + e].astype(jnp.int32)
    slot_c = rows_ref[53:54].astype(jnp.int32)
    both = jnp.minimum(slot_a, slot_c) >= 0
    code = jnp.where(both, (slot_a >> 4) * CAM + slot_c, -1)
    onehot = (lanes_of(code, 256) == iota((256, LANES), 0)).astype(F32).astype(BF)
    mask = (lanes_of(slot_a & 15, 16) == iota((16, LANES), 0)).astype(F32).astype(BF)
    n = GROUP * 144
    for g in range(9 // GROUP):
        parts = []
        for h in range(2):
            for j in range(g * GROUP, (g + 1) * GROUP):
                for i in range(9):
                    parts.append(lanes_of(prod[h, j, i : i + 1], 16).astype(BF) * mask)
        left = jnp.concatenate(parts, axis=0)
        got = lax.dot_general(left, onehot, NT, preferred_element_type=F32)
        acc[e, g * n : (g + 1) * n, :] += got[:n] + got[n:]


def assemble(e, read, flag, damp_ref, out_ref, stage, wide_ref):
    source = iota((640, 640), 0)
    place = iota((640, 640), 1) == 9 * (source % CAM) + source // CAM
    place = (place & (source < TILE)).astype(F32).astype(BF)
    lane = iota((144, PTS), 1)
    for u in range(4):
        base = (u // 2) * 128
        tiles = []
        for jj in range(5):
            even = read(2 * jj, base)
            if u % 2:
                even = pltpu.roll(even, 64, 1)
            if jj < 4:
                odd = read(2 * jj + 1, base)
                if u % 2 == 0:
                    odd = pltpu.roll(odd, 64, 1)
                even = jnp.where(lane < CAM, even, odd)
            tiles.append(even)
        full = jnp.concatenate(tiles, axis=1)
        high = full.astype(BF)
        wide_ref[144 * u : 144 * u + 144] = high
        wide_ref[TILE + 144 * u : TILE + 144 * u + 144] = (full - high.astype(F32)).astype(BF)
    got = jnp.dot(wide_ref[...], place, preferred_element_type=F32)
    got = got[:TILE] + got[TILE:]
    for u in range(4):
        for tile in range(5):
            for i in range(9):
                at = 144 * u + 16 * i
                piece = got[at : at + 16, 128 * tile : 128 * tile + 128]
                stage[pl.ds(TILE * tile + 144 * u + i, 16, stride=9), :] = piece
    for tile in range(5):
        wide = min(128, TILE - 128 * tile)
        block = stage[TILE * tile : TILE * tile + TILE, 0:wide]
        out_ref[e, :, 128 * tile : 128 * tile + wide] = block

    @pl.when(flag == 1)
    def _():
        same = iota((TILE, TILE), 0) == iota((TILE, TILE), 1)
        out_ref[e] += jnp.where(same, jnp.broadcast_to(damp_ref[...], (TILE, TILE)), 0.0)


def spread_kernel(flag_ref, rows_ref, damp_ref, behind, out_ref, token, prod, acc, stage, wide_ref):
    step = pl.program_id(0)

    @pl.when(step == 0)
    def _():
        acc[...] = jnp.zeros_like(acc)

    for e in range(2):
        add_products(e, rows_ref, prod, acc)

    @pl.when(step == pl.num_programs(0) - 1)
    def _():
        for e in range(2):

            def read(j, base):
                return acc[e, 144 * j : 144 * j + 144, base : base + 128]

            assemble(e, read, flag_ref[e], damp_ref, out_ref, stage, wide_ref)
        token[...] = jnp.zeros_like(token)


def spread(flags, rows, damp, behind):
    return pl.pallas_call(
        spread_kernel,
        grid=(NDEV // SRC,),
        in_specs=[
            pl.BlockSpec(memory_space=pltpu.SMEM),
            pl.BlockSpec((ROWS, LANES), lambda s: (0, s)),
            whole(1, TILE),
            ANY,
        ],
        out_specs=[whole(2, TILE, TILE), whole(8, 128)],
        out_shape=[
            jax.ShapeDtypeStruct((2, TILE, TILE), F32),
            jax.ShapeDtypeStruct((8, 128), F32),
        ],
        scratch_shapes=[
            pltpu.VMEM((2, 9, 16, LANES), F32),
            pltpu.VMEM((2, 1296, 256), F32),
            pltpu.VMEM((5 * TILE, 128), F32),
            pltpu.VMEM((2 * TILE, 640), BF),
        ],
        name="spread",
        **settings(45, 60),
    )(flags, rows, damp, behind)


def finish_kernel(in_ref, behind, step_ref, res_ref, dir_ref):
    pieces = []
    for r in range(NROW):
        pieces.append(jnp.sum(in_ref[NCL * r : NCL * r + NCL], axis=0))
    lane = iota((16, 128), 1)
    image = jnp.concatenate([jnp.where(iota((16, 128), 0) < 9, p, 0.0) for p in pieces], axis=1)
    both = []
    for c in range(NCL):
        rows = jnp.concatenate([in_ref[NCL * r + c, 9:12, :] for r in range(6)], axis=0)
        both.append(rows)
    wide = iota((18, 128), 1)
    both = [
        jnp.where(wide < CAM, both[2 * g], pltpu.roll(both[2 * g + 1], CAM, 1))
        for g in range(NCL // 2)
    ]
    both = jnp.concatenate(both, axis=1)
    pad = jnp.zeros((7, NCL * CAM), F32)
    rhs = jnp.concatenate([both[0:8], both[16:17], pad], axis=0)
    diag = jnp.concatenate([both[8:16], both[17:18], pad + 1.0], axis=0)
    start = rhs / diag
    rz = jnp.sum(rhs * start)
    alpha = rz / jnp.sum(start * image)
    residual = rhs - alpha * image
    second = residual / diag
    beta = jnp.sum(residual * second) / rz
    values = (alpha * start, residual, second + beta * start)
    for r in range(9):
        at = 128 * r + lane
        camera = at // 9
        keep = at - 9 * camera == iota((16, 128), 0)
        camera = camera[0:8]
        for value, ref in zip(values, (step_ref, res_ref, dir_ref)):
            for g in range(NCL // 2):
                part = value[:, 128 * g : 128 * g + 128]
                top = jnp.take_along_axis(part[0:8], camera, axis=1)
                low = jnp.take_along_axis(part[8:16], camera, axis=1)
                found = jnp.where(keep, jnp.concatenate([top, low], axis=0), 0.0)
                ref[9 * g + r : 9 * g + r + 1, :] = jnp.sum(found, axis=0, keepdims=True)


def finish(incoming, behind):
    return pl.pallas_call(
        finish_kernel,
        grid=(1,),
        in_specs=[whole(NDEV, 16, 128), ANY],
        out_specs=[whole(72, 128)] * 3,
        out_shape=[jax.ShapeDtypeStruct((72, 128), F32)] * 3,
        name="finish",
        **settings(3, 60),
    )(incoming, behind)


def shards(jac_cam, jac_pt, resid, point_damp, cam_damp, obs_cluster, obs_slot):
    my_row = lax.axis_index("row")
    my_col = lax.axis_index("col")
    flags = (2 * my_row + jnp.arange(2) == my_col).astype(jnp.int32)
    flags = jnp.concatenate([flags, my_row[None].astype(jnp.int32)])
    damp = jnp.pad(cam_damp.reshape(CAM, 9).T, ((0, 0), (0, 128 - CAM)), constant_values=1.0)
    zeros = jnp.zeros((8, 128), F32)
    damp = jnp.concatenate([zeros, damp[0:8], zeros[0:1], damp[8:9], zeros[0:6]], axis=0)
    dense, found = points(
        jac_cam.transpose(1, 0, 2), jac_pt.transpose(1, 0, 2), resid, point_damp, obs_cluster.T,
        obs_slot,
    )
    incoming = exchange(pack(dense, found).reshape(NDEV, SENT, PTS))
    rows, share = cg_part(flags, incoming, damp)
    shares = exchange(share)
    tiles, token = spread(flags, rows, cam_damp, share)
    step, residual, direction = finish(shares, token)
    return (tiles[:, None], step.reshape(-1), residual.reshape(-1), direction.reshape(-1))


def solution(mesh):
    placed = (
        P(None, None, AXES),
        P(None, None, AXES),
        P(None, None, AXES),
        P(None, AXES),
        P("col", None),
        P(AXES, None),
        P(None, AXES),
    )
    return jax.shard_map(
        shards,
        mesh=mesh,
        in_specs=placed,
        out_specs=(P("row", "col", None, None), P(), P(), P()),
        check_vma=False,
    )
```

```python
import functools

import jax
import jax.numpy as jnp
from jax import lax
from jax.experimental import pallas as pl
from jax.experimental.pallas import tpu as pltpu
from jax.sharding import PartitionSpec as P

KOBS = 8
NCL = 16
CAP = 96
CAM = 64
TILE = 576
NROW = 8
NDEV = 128
PTS = 128
AXES = ("row", "col")
BF = jnp.bfloat16
F8 = jnp.float8_e4m3fn
F32 = jnp.float32
NT = (((1,), (1,)), ((), ()))
MIB = 1 << 20
SRC = 32
PAIRS = 2
LANES = SRC * CAP
GROUP = 3
ANY = pl.BlockSpec(memory_space=pl.ANY)


def iota(shape, dim):
    return lax.broadcasted_iota(jnp.int32, shape, dim)


def whole(*shape):
    return pl.BlockSpec(shape, lambda *_: (0,) * len(shape))


def settings(micros, mib):
    return dict(
        compiler_params=pltpu.CompilerParams(vmem_limit_bytes=mib * MIB),
        cost_estimate=pl.CostEstimate(
            flops=micros * 10**9, bytes_accessed=10**6, transcendentals=0
        ),
    )


def lanes_of(row, n):
    return jnp.broadcast_to(row, (n, row.shape[1]))


def whitened(jp, rs, damp):
    def inner(a, b):
        return jnp.sum(jp[0][a] * jp[0][b] + jp[1][a] * jp[1][b], axis=0, keepdims=True)

    laa = jnp.sqrt(inner(0, 0) + damp[0:1])
    lba = inner(1, 0) / laa
    lca = inner(2, 0) / laa
    lbb = jnp.sqrt(inner(1, 1) + damp[1:2] - lba * lba)
    lcb = (inner(2, 1) - lca * lba) / lbb
    lcc = jnp.sqrt(inner(2, 2) + damp[2:3] - lca * lca - lcb * lcb)

    def solve(a, b, c):
        x = a / laa
        y = (b - lba * x) / lbb
        return [x, y, (c - lca * x - lcb * y) / lcc]

    u = [solve(*jp[m]) for m in range(2)]
    grad = [
        jnp.sum(jp[0][a] * rs[0] + jp[1][a] * rs[1], axis=0, keepdims=True) for a in range(3)
    ]
    w = solve(*grad)
    q = [u[m][0] * w[0] + u[m][1] * w[1] + u[m][2] * w[2] - rs[m] for m in range(2)]
    return u, q


def hot(code, n):
    codes = lanes_of(code.astype(F32), n).astype(BF)
    ids = iota((n, code.shape[1]), 0).astype(F32).astype(BF)
    return jnp.where(codes == ids, jnp.ones((), BF), jnp.zeros((), BF))


def three(value):
    a = value.astype(BF)
    rest = value - a.astype(F32)
    b = rest.astype(BF)
    return jnp.concatenate([a, b, (rest - b.astype(F32)).astype(BF)], axis=0)


def chosen(named):
    upto = (iota((PTS, PTS), 0) <= iota((PTS, PTS), 1)).astype(F32).astype(BF)
    counts = jnp.dot(named.astype(BF), upto, preferred_element_type=F32)
    lane = iota(named.shape, 1)
    at = jnp.zeros(named.shape, jnp.int32)
    for jump in (64, 32, 16, 8, 4, 2, 1):
        seen = jnp.take_along_axis(counts, at + (jump - 1), axis=1)
        at = jnp.where(seen <= lane.astype(F32), at + jump, at)
    return jnp.where(lane.astype(F32) < counts[:, PTS - 1 : PTS], at, PTS)


def points_part(jc, jp, rs, damp, cl_ref, slot_ref, dense, found_ref, fields):
    cl, slot = cl_ref[...], slot_ref[...]
    u, q = whitened(
        [[jp[m * 3 + a] for a in range(3)] for m in range(2)],
        [rs[:, m, :] for m in range(2)],
        damp[...],
    )
    j0, j1 = jc[0], jc[9]
    top = jnp.maximum(jnp.abs(j0), jnp.abs(j1))
    some = top > 0.0
    safe = jnp.where(some, top, 1.0)
    x, y = j0 / safe, j1 / safe
    length = jnp.where(some, jnp.sqrt(x * x + y * y), 1.0)
    cs = jnp.where(some, x / length, 1.0)
    sn = jnp.where(some, y / length, 0.0)
    for i in range(9):
        a, b = jc[i], jc[9 + i]
        fields[i] = cs * a + sn * b
        if i:
            fields[8 + i] = cs * b - sn * a
    turned = [[], []]
    for a in range(3):
        turned[0].append(cs * u[0][a] + sn * u[1][a])
        turned[1].append(cs * u[1][a] - sn * u[0][a])
        fields[17 + a] = turned[0][a]
        fields[20 + a] = turned[1][a]
    fields[23] = slot.astype(F32)
    fields[24] = cs * q[0] + sn * q[1]
    fields[25] = cs * q[1] - sn * q[0]
    fields[26] = 1.0 - sum(v * v for v in turned[0])
    fields[27] = -2.0 * sum(v * w for v, w in zip(*turned))
    fields[28] = 1.0 - sum(v * v for v in turned[1])
    for e in range(2):
        ids = 2 * iota((NROW, PTS), 0) + e
        hits = [lanes_of(cl[k : k + 1], NROW) == ids for k in range(KOBS)]
        for f in range(29):
            value = jnp.full((NROW, PTS), -1.0 if f == 23 else 0.0, F32)
            for k in range(KOBS):
                value = jnp.where(hits[k], lanes_of(fields[f, k : k + 1, :], NROW), value)
            dense[f, e] = value
        found_ref[e] = chosen((dense[23, e] >= 0.0).astype(F32))


def mixed(side, mine, on):
    out = []
    for m in range(2):
        for n in range(2):
            v = sum(side[17 + 3 * m + a] * mine[17 + 3 * n + a] for a in range(3))
            out.append(on - v if m == n else -v)
    return out


def pack_kernel(jc, jp, rs, damp, cl, slot, out_ref, dense, found_ref, fields, kept):
    step = pl.program_id(0)

    @pl.when(step == 0)
    def _():
        points_part(jc, jp, rs, damp, cl, slot, dense, found_ref, fields)

    for part in range(PAIRS):
        pack_pair(step * PAIRS + part, part, out_ref, dense, found_ref, kept)


def pack_pair(pair, part, out_ref, dense, found_ref, kept):
    lane = iota((NROW, PTS), 1)
    zero = jnp.zeros((NROW, PTS), F32)
    flat = out_ref.reshape(NROW * 2 * PAIRS * SENT, PTS)
    for ec in range(2):
        found = lanes_of(found_ref[ec, pl.ds(pair, 1), :], NROW)
        pick = jnp.minimum(found, PTS - 1)
        side = [
            [jnp.take_along_axis(dense[f, e], pick, axis=1) for f in range(24)] for e in range(2)
        ]
        for f in range(29):
            if f < 24:
                kept[2 * part + ec, f] = side[ec][f]
            else:
                kept[2 * part + ec, f] = jnp.take_along_axis(dense[f, ec], pick, axis=1)
        mine = [lanes_of(kept[2 * part + ec, f, pl.ds(pair, 1), :], NROW) for f in range(29)]
        rows = side[0][0:16] + side[1][0:16] + mine[0:16]
        rows += [side[0][16], side[1][16], mine[16], side[0][23], side[1][23]]
        rows.append(jnp.where(found < PTS, mine[23], -1.0))
        rows += mine[24:26]
        extra = []
        for e in range(2):
            same = jnp.where(iota((NROW, PTS), 0) == pair, float(e == ec), 0.0)
            extra += mixed(side[e], mine, same)
        extra += mine[26:29]
        for at, row in enumerate(rows):
            v, x = at // 16, at % 16
            rest = pltpu.roll(extra[x], 96 - 32 * v, 1) if v < 3 and x < 11 else zero
            at = SENT * (2 * part + ec) + at
            flat[pl.ds(at, NROW, stride=2 * PAIRS * SENT), :] = jnp.where(lane < CAP, row, rest)


def pack(*args):
    return pl.pallas_call(
        pack_kernel,
        grid=(NROW // PAIRS,),
        in_specs=[whole(*a.shape) for a in args],
        out_specs=pl.BlockSpec((NROW, 2 * PAIRS, SENT, PTS), lambda g: (0, g, 0, 0)),
        out_shape=jax.ShapeDtypeStruct((NROW, NCL, SENT, PTS), F32),
        scratch_shapes=[
            pltpu.VMEM((29, 2, NROW, PTS), F32),
            pltpu.VMEM((2, NROW, PTS), jnp.int32),
            pltpu.VMEM((29, KOBS, PTS), F32),
            pltpu.VMEM((2 * PAIRS, 29, NROW, PTS), F32),
        ],
        name="pack",
        **settings(8, 60),
    )(*args)


def exchange(value):
    return lax.all_to_all(value, AXES, split_axis=0, concat_axis=0, tiled=True)


ROWS = 72
SENT = 56


def lay(in_ref, rows_ref):
    lane = iota((16, PTS), 1)
    full = iota((ROWS, PTS), 1)
    for quarter in range(SRC // 4):
        pieces = []
        for s in range(4):
            block = in_ref[quarter * 4 + s]
            part = [pltpu.roll(block[16 * v : 16 * v + 16], 32 + 32 * v, 1) for v in range(3)]
            rest = jnp.where(lane < 32, part[0], jnp.where(lane < 64, part[1], part[2]))
            pieces.append(jnp.concatenate([block, rest], axis=0))
        r1, r2 = pltpu.roll(pieces[1], 96, 1), pltpu.roll(pieces[2], 64, 1)
        r3 = pltpu.roll(pieces[3], 32, 1)
        base = quarter * 384
        rows_ref[:, base : base + 128] = jnp.where(full < 96, pieces[0], r1)
        rows_ref[:, base + 128 : base + 256] = jnp.where(full < 64, r1, r2)
        rows_ref[:, base + 256 : base + 384] = jnp.where(full < 32, r2, r3)


def jacobian(rows_ref, which):
    at = 16 * which
    first = iota((8, LANES), 0) == 0
    a1 = jnp.where(first, 0.0, rows_ref[at + 8 : at + 16])
    return rows_ref[at : at + 8], a1, rows_ref[at + 8 : at + 9], rows_ref[48 + which : 49 + which]


def cg_kernel(
    flag_ref, in_ref, damp_ref, rows_ref, out_ref, scale_ref, keep, hits, sums, image, largest
):
    step = pl.program_id(0)
    steps = pl.num_programs(0)

    @pl.when(step == 0)
    def _():
        sums[...] = jnp.zeros_like(sums)
        largest[...] = jnp.zeros_like(largest)

    lay(in_ref, rows_ref)
    top = [jnp.max(jnp.abs(rows_ref[8 * v : 8 * v + 8]), axis=0, keepdims=True) for v in range(6)]
    top.append(jnp.max(jnp.abs(rows_ref[48:51]), axis=0, keepdims=True))
    largest[...] = jnp.maximum(largest[...], functools.reduce(jnp.maximum, top))
    a0, a1, l0, l1 = jacobian(rows_ref, 2)
    q0, q1 = rows_ref[54:55], rows_ref[55:56]
    m0, m1, m2 = rows_ref[64:65], rows_ref[65:66], rows_ref[66:67]
    terms = [
        a0 * lanes_of(q0, 8) + a1 * lanes_of(q1, 8),
        a0 * a0 * lanes_of(m0, 8) + a0 * a1 * lanes_of(m1, 8) + a1 * a1 * lanes_of(m2, 8),
        l0 * q0 + l1 * q1,
        l0 * l0 * m0 + l0 * l1 * m1 + l1 * l1 * m2,
        jnp.zeros((14, LANES), F32),
    ]
    slot = rows_ref[53:54].astype(jnp.int32)
    hit = hot(slot, 128)
    hits[step] = hit
    keep[step] = rows_ref[...]
    sums[...] += lax.dot_general(
        three(jnp.concatenate(terms, axis=0)), hit, NT, preferred_element_type=F32
    )

    @pl.when(step == steps - 1)
    def _():
        damp = damp_ref[...]
        total = sums[0:24] + sums[32:56] + sums[64:88] + damp
        sums[0:24] = total
        x8, x9 = total[0:8] / total[8:16], total[16:17] / total[17:18]
        x = three(jnp.concatenate([x8, x9, jnp.zeros((7, 128), F32)], axis=0))
        image[...] = jnp.zeros_like(image)

        @pl.loop(0, steps, unroll=4)
        def _(at):
            rows = keep.at[at]
            got = jnp.dot(x, hits[at], preferred_element_type=F32)
            got = got[0:16] + got[16:32] + got[32:48]
            a0, a1, l0, l1 = jacobian(rows, 2)
            v0 = jnp.sum(a0 * got[0:8], axis=0, keepdims=True) + l0 * got[8:9]
            v1 = jnp.sum(a1 * got[0:8], axis=0, keepdims=True) + l1 * got[8:9]
            for e in range(2):
                m = [rows[56 + 4 * e + n : 57 + 4 * e + n] for n in range(4)]
                z0, z1 = m[0] * v0 + m[1] * v1, m[2] * v0 + m[3] * v1
                a0, a1, l0, l1 = jacobian(rows, e)
                out8 = a0 * lanes_of(z0, 8) + a1 * lanes_of(z1, 8)
                terms = [out8, l0 * z0 + l1 * z1, jnp.zeros((7, LANES), F32)]
                slot = rows[51 + e : 52 + e].astype(jnp.int32)
                slot = jnp.where(slot >= 0, slot + CAM * e, -1)
                hit = hot(slot, 128)
                image[...] += lax.dot_general(
                    three(jnp.concatenate(terms, axis=0)), hit, NT, preferred_element_type=F32
                )

        y = image[0:16] + image[16:32] + image[32:48]
        own = iota((16, 128), 1) < CAM
        extra = jnp.concatenate([damp[8:16] * x8, damp[17:18] * x9, jnp.zeros((7, 128), F32)], axis=0)
        extra = jnp.where(own, extra, 0.0)
        y += jnp.where(flag_ref[0] == 1, extra, 0.0)
        y += jnp.where(flag_ref[1] == 1, pltpu.roll(extra, CAM, 1), 0.0)
        part = sums[pl.ds(3 * flag_ref[2], 3), :]
        block = jnp.concatenate([y[0:9], part, jnp.zeros((4, 128), F32)], axis=0)
        out_ref[...] = jnp.broadcast_to(block[None], (NDEV, 16, 128))
        top = jnp.maximum(jnp.max(largest[...], keepdims=True), 1e-15)
        scale = jnp.broadcast_to(32768.0 / (top * top), (8, 128))
        scale_ref[...] = jnp.where(iota((8, 128), 0) == 1, 1.0 / scale, scale)


def cg_part(flags, incoming, damp):
    steps = NDEV // SRC
    return pl.pallas_call(
        cg_kernel,
        grid=(steps,),
        in_specs=[
            pl.BlockSpec(memory_space=pltpu.SMEM),
            pl.BlockSpec((SRC, SENT, PTS), lambda s: (s, 0, 0)),
            whole(24, 128),
        ],
        out_specs=[
            pl.BlockSpec((ROWS, LANES), lambda s: (0, s)),
            whole(NDEV, 16, 128),
            whole(8, 128),
        ],
        out_shape=[
            jax.ShapeDtypeStruct((ROWS, steps * LANES), F32),
            jax.ShapeDtypeStruct((NDEV, 16, 128), F32),
            jax.ShapeDtypeStruct((8, 128), F32),
        ],
        scratch_shapes=[
            pltpu.VMEM((steps, ROWS, LANES), F32),
            pltpu.VMEM((steps, 128, LANES), BF),
            pltpu.VMEM((96, 128), F32),
            pltpu.VMEM((48, 128), F32),
            pltpu.VMEM((1, LANES), F32),
        ],
        name="cg",
        **settings(6, 60),
    )(flags, incoming, damp)


def add_products(e, rows_ref, scale_ref, prod, acc):
    scale = scale_ref[0:1, 0:1]

    def split(value):
        high = value.astype(BF).astype(F32)
        return high, value - high

    a0, a1, last0, last1 = jacobian(rows_ref, e)
    cam0, cam1, cam_last0, cam_last1 = jacobian(rows_ref, 2)
    t, t_last = [], []
    for m in range(2):
        at = 56 + 4 * e + 2 * m
        m0, m1 = rows_ref[at : at + 1] * scale, rows_ref[at + 1 : at + 2] * scale
        t.append(lanes_of(m0, 8) * cam0 + lanes_of(m1, 8) * cam1)
        t_last.append(m0 * cam_last0 + m1 * cam_last1)
    for j in range(9):
        t0 = t[0][j : j + 1] if j < 8 else t_last[0]
        t1 = t[1][j : j + 1] if j < 8 else t_last[1]
        high, low = split(a0 * lanes_of(t0, 8) + a1 * lanes_of(t1, 8))
        prod[0, j, 0:8] = high
        prod[1, j, 0:8] = low
        high, low = split(last0 * t0 + last1 * t1)
        prod[0, j, 8:9] = high
        prod[1, j, 8:9] = low
    slot_a = rows_ref[51 + e : 52 + e].astype(jnp.int32)
    slot_c = rows_ref[53:54].astype(jnp.int32)
    both = jnp.minimum(slot_a, slot_c) >= 0
    code = jnp.where(both, (slot_a >> 4) * CAM + slot_c, -1)
    onehot = hot(code, 256)
    mask = hot(slot_a & 15, 16)
    n = GROUP * 144
    onehot8 = onehot.astype(F8)
    for g in range(9 // GROUP):
        parts = [[], []]
        for h in range(2):
            for j in range(g * GROUP, (g + 1) * GROUP):
                for i in range(9):
                    parts[h].append(lanes_of(prod[h, j, i : i + 1], 16).astype(BF) * mask)
        high = jnp.concatenate(parts[0], axis=0)
        low = jnp.concatenate(parts[1], axis=0).astype(F8)
        got = lax.dot_general(high, onehot, NT, preferred_element_type=F32)
        rest = lax.dot_general(low, onehot8, NT, preferred_element_type=F32)
        acc[e, g * n : (g + 1) * n, :] += got + rest


def assemble(e, read, undo, flag, damp_ref, out_ref, stage, wide_ref):
    source = iota((640, 640), 0)
    place = iota((640, 640), 1) == 9 * (source % CAM) + source // CAM
    place = (place & (source < TILE)).astype(F32).astype(BF)
    lane = iota((144, PTS), 1)
    for u in range(4):
        base = (u // 2) * 128
        tiles = []
        for jj in range(5):
            even = read(2 * jj, base)
            if u % 2:
                even = pltpu.roll(even, 64, 1)
            if jj < 4:
                odd = read(2 * jj + 1, base)
                if u % 2 == 0:
                    odd = pltpu.roll(odd, 64, 1)
                even = jnp.where(lane < CAM, even, odd)
            tiles.append(even)
        full = jnp.concatenate(tiles, axis=1) * undo
        high = full.astype(BF)
        wide_ref[144 * u : 144 * u + 144] = high
        wide_ref[TILE + 144 * u : TILE + 144 * u + 144] = (full - high.astype(F32)).astype(BF)
    got = jnp.dot(wide_ref[...], place, preferred_element_type=F32)
    got = got[:TILE] + got[TILE:]
    for u in range(4):
        for tile in range(5):
            for i in range(9):
                at = 144 * u + 16 * i
                piece = got[at : at + 16, 128 * tile : 128 * tile + 128]
                stage[pl.ds(TILE * tile + 144 * u + i, 16, stride=9), :] = piece
    for tile in range(5):
        wide = min(128, TILE - 128 * tile)
        block = stage[TILE * tile : TILE * tile + TILE, 0:wide]
        out_ref[e, :, 128 * tile : 128 * tile + wide] = block

    @pl.when(flag == 1)
    def _():
        same = iota((TILE, TILE), 0) == iota((TILE, TILE), 1)
        out_ref[e] += jnp.where(same, jnp.broadcast_to(damp_ref[...], (TILE, TILE)), 0.0)


def spread_kernel(
    flag_ref, rows_ref, scale_ref, damp_ref, behind, out_ref, token, prod, acc, stage, wide_ref
):
    step = pl.program_id(0)

    @pl.when(step == 0)
    def _():
        acc[...] = jnp.zeros_like(acc)

    for e in range(2):
        add_products(e, rows_ref, scale_ref, prod, acc)

    @pl.when(step == pl.num_programs(0) - 1)
    def _():
        for e in range(2):

            def read(j, base):
                return acc[e, 144 * j : 144 * j + 144, base : base + 128]

            assemble(e, read, scale_ref[1:2, 0:1], flag_ref[e], damp_ref, out_ref, stage, wide_ref)
        token[...] = jnp.zeros_like(token)


def spread(flags, rows, scale, damp, behind):
    return pl.pallas_call(
        spread_kernel,
        grid=(NDEV // SRC,),
        in_specs=[
            pl.BlockSpec(memory_space=pltpu.SMEM),
            pl.BlockSpec((ROWS, LANES), lambda s: (0, s)),
            whole(8, 128),
            whole(1, TILE),
            ANY,
        ],
        out_specs=[whole(2, TILE, TILE), whole(8, 128)],
        out_shape=[
            jax.ShapeDtypeStruct((2, TILE, TILE), F32),
            jax.ShapeDtypeStruct((8, 128), F32),
        ],
        scratch_shapes=[
            pltpu.VMEM((2, 9, 16, LANES), F32),
            pltpu.VMEM((2, 1296, 256), F32),
            pltpu.VMEM((5 * TILE, 128), F32),
            pltpu.VMEM((2 * TILE, 640), BF),
        ],
        name="spread",
        **settings(45, 60),
    )(flags, rows, scale, damp, behind)


def finish_kernel(in_ref, behind, step_ref, res_ref, dir_ref):
    pieces = []
    for r in range(NROW):
        pieces.append(jnp.sum(in_ref[NCL * r : NCL * r + NCL], axis=0))
    lane = iota((16, 128), 1)
    image = jnp.concatenate([jnp.where(iota((16, 128), 0) < 9, p, 0.0) for p in pieces], axis=1)
    both = []
    for c in range(NCL):
        rows = jnp.concatenate([in_ref[NCL * r + c, 9:12, :] for r in range(6)], axis=0)
        both.append(rows)
    wide = iota((18, 128), 1)
    both = [
        jnp.where(wide < CAM, both[2 * g], pltpu.roll(both[2 * g + 1], CAM, 1))
        for g in range(NCL // 2)
    ]
    both = jnp.concatenate(both, axis=1)
    pad = jnp.zeros((7, NCL * CAM), F32)
    rhs = jnp.concatenate([both[0:8], both[16:17], pad], axis=0)
    diag = jnp.concatenate([both[8:16], both[17:18], pad + 1.0], axis=0)
    start = rhs / diag
    rz = jnp.sum(rhs * start)
    alpha = rz / jnp.sum(start * image)
    residual = rhs - alpha * image
    second = residual / diag
    beta = jnp.sum(residual * second) / rz
    values = (alpha * start, residual, second + beta * start)
    for r in range(9):
        at = 128 * r + lane
        camera = at // 9
        keep = at - 9 * camera == iota((16, 128), 0)
        camera = camera[0:8]
        for value, ref in zip(values, (step_ref, res_ref, dir_ref)):
            for g in range(NCL // 2):
                part = value[:, 128 * g : 128 * g + 128]
                top = jnp.take_along_axis(part[0:8], camera, axis=1)
                low = jnp.take_along_axis(part[8:16], camera, axis=1)
                found = jnp.where(keep, jnp.concatenate([top, low], axis=0), 0.0)
                ref[9 * g + r : 9 * g + r + 1, :] = jnp.sum(found, axis=0, keepdims=True)


def finish(incoming, behind):
    return pl.pallas_call(
        finish_kernel,
        grid=(1,),
        in_specs=[whole(NDEV, 16, 128), ANY],
        out_specs=[whole(72, 128)] * 3,
        out_shape=[jax.ShapeDtypeStruct((72, 128), F32)] * 3,
        name="finish",
        **settings(3, 60),
    )(incoming, behind)


def shards(jac_cam, jac_pt, resid, point_damp, cam_damp, obs_cluster, obs_slot):
    my_row = lax.axis_index("row")
    my_col = lax.axis_index("col")
    flags = (2 * my_row + jnp.arange(2) == my_col).astype(jnp.int32)
    flags = jnp.concatenate([flags, my_row[None].astype(jnp.int32)])
    damp = jnp.pad(cam_damp.reshape(CAM, 9).T, ((0, 0), (0, 128 - CAM)), constant_values=1.0)
    zeros = jnp.zeros((8, 128), F32)
    damp = jnp.concatenate([zeros, damp[0:8], zeros[0:1], damp[8:9], zeros[0:6]], axis=0)
    packed = pack(
        jac_cam.transpose(1, 0, 2), jac_pt.transpose(1, 0, 2), resid, point_damp, obs_cluster.T,
        obs_slot,
    )
    incoming = exchange(packed.reshape(NDEV, SENT, PTS))
    rows, share, scale = cg_part(flags, incoming, damp)
    shares = exchange(share)
    tiles, token = spread(flags, rows, scale, cam_damp, share)
    step, residual, direction = finish(shares, token)
    return (tiles[:, None], step.reshape(-1), residual.reshape(-1), direction.reshape(-1))


def solution(mesh):
    placed = (
        P(None, None, AXES),
        P(None, None, AXES),
        P(None, None, AXES),
        P(None, AXES),
        P("col", None),
        P(AXES, None),
        P(None, AXES),
    )
    return jax.shard_map(
        shards,
        mesh=mesh,
        in_specs=placed,
        out_specs=(P("row", "col", None, None), P(), P(), P()),
        check_vma=False,
    )
```

```python
import functools

import jax
import jax.numpy as jnp
from jax import lax
from jax.experimental import pallas as pl
from jax.experimental.pallas import tpu as pltpu
from jax.sharding import PartitionSpec as P

KOBS = 8
NCL = 16
CAP = 96
CAM = 64
TILE = 576
NROW = 8
NDEV = 128
PTS = 128
AXES = ("row", "col")
BF = jnp.bfloat16
F8 = jnp.float8_e4m3fn
F32 = jnp.float32
NT = (((1,), (1,)), ((), ()))
MIB = 1 << 20
SRC = 32
PAIRS = 2
LANES = SRC * CAP
GROUP = 3
ANY = pl.BlockSpec(memory_space=pl.ANY)


def iota(shape, dim):
    return lax.broadcasted_iota(jnp.int32, shape, dim)


def whole(*shape):
    return pl.BlockSpec(shape, lambda *_: (0,) * len(shape))


def settings(micros, mib):
    return dict(
        compiler_params=pltpu.CompilerParams(vmem_limit_bytes=mib * MIB),
        cost_estimate=pl.CostEstimate(
            flops=micros * 10**9, bytes_accessed=10**6, transcendentals=0
        ),
    )


def lanes_of(row, n):
    return jnp.broadcast_to(row, (n, row.shape[1]))


def whitened(jp, rs, damp):
    def inner(a, b):
        return jnp.sum(jp[0][a] * jp[0][b] + jp[1][a] * jp[1][b], axis=0, keepdims=True)

    laa = jnp.sqrt(inner(0, 0) + damp[0:1])
    lba = inner(1, 0) / laa
    lca = inner(2, 0) / laa
    lbb = jnp.sqrt(inner(1, 1) + damp[1:2] - lba * lba)
    lcb = (inner(2, 1) - lca * lba) / lbb
    lcc = jnp.sqrt(inner(2, 2) + damp[2:3] - lca * lca - lcb * lcb)

    def solve(a, b, c):
        x = a / laa
        y = (b - lba * x) / lbb
        return [x, y, (c - lca * x - lcb * y) / lcc]

    u = [solve(*jp[m]) for m in range(2)]
    grad = [
        jnp.sum(jp[0][a] * rs[0] + jp[1][a] * rs[1], axis=0, keepdims=True) for a in range(3)
    ]
    w = solve(*grad)
    q = [u[m][0] * w[0] + u[m][1] * w[1] + u[m][2] * w[2] - rs[m] for m in range(2)]
    return u, q


def hot(code, n):
    codes = lanes_of(code.astype(F32), n).astype(BF)
    ids = iota((n, code.shape[1]), 0).astype(F32).astype(BF)
    return jnp.where(codes == ids, jnp.ones((), BF), jnp.zeros((), BF))


def three(value):
    a = value.astype(BF)
    rest = value - a.astype(F32)
    b = rest.astype(BF)
    return jnp.concatenate([a, b, (rest - b.astype(F32)).astype(BF)], axis=0)


def chosen(named):
    upto = (iota((PTS, PTS), 0) <= iota((PTS, PTS), 1)).astype(F32).astype(BF)
    counts = jnp.dot(named.astype(BF), upto, preferred_element_type=F32)
    lane = iota(named.shape, 1)
    at = jnp.zeros(named.shape, jnp.int32)
    for jump in (64, 32, 16, 8, 4, 2, 1):
        seen = jnp.take_along_axis(counts, at + (jump - 1), axis=1)
        at = jnp.where(seen <= lane.astype(F32), at + jump, at)
    return jnp.where(lane.astype(F32) < counts[:, PTS - 1 : PTS], at, PTS)


def points_part(jc, jp, rs, damp, cl_ref, slot_ref, dense, found_ref, fields):
    cl, slot = cl_ref[...], slot_ref[...]
    u, q = whitened(
        [[jp[m * 3 + a] for a in range(3)] for m in range(2)],
        [rs[:, m, :] for m in range(2)],
        damp[...],
    )
    j0, j1 = jc[0], jc[9]
    top = jnp.maximum(jnp.abs(j0), jnp.abs(j1))
    some = top > 0.0
    safe = jnp.where(some, top, 1.0)
    x, y = j0 / safe, j1 / safe
    length = jnp.where(some, jnp.sqrt(x * x + y * y), 1.0)
    cs = jnp.where(some, x / length, 1.0)
    sn = jnp.where(some, y / length, 0.0)
    for i in range(9):
        a, b = jc[i], jc[9 + i]
        fields[i] = cs * a + sn * b
        if i:
            fields[8 + i] = cs * b - sn * a
    turned = [[], []]
    for a in range(3):
        turned[0].append(cs * u[0][a] + sn * u[1][a])
        turned[1].append(cs * u[1][a] - sn * u[0][a])
        fields[17 + a] = turned[0][a]
        fields[20 + a] = turned[1][a]
    fields[23] = slot.astype(F32)
    fields[24] = cs * q[0] + sn * q[1]
    fields[25] = cs * q[1] - sn * q[0]
    fields[26] = 1.0 - sum(v * v for v in turned[0])
    fields[27] = -2.0 * sum(v * w for v, w in zip(*turned))
    fields[28] = 1.0 - sum(v * v for v in turned[1])
    for e in range(2):
        ids = 2 * iota((NROW, PTS), 0) + e
        hits = [lanes_of(cl[k : k + 1], NROW) == ids for k in range(KOBS)]
        for f in range(29):
            value = jnp.full((NROW, PTS), -1.0 if f == 23 else 0.0, F32)
            for k in range(KOBS):
                value = jnp.where(hits[k], lanes_of(fields[f, k : k + 1, :], NROW), value)
            dense[f, e] = value
        found_ref[e] = chosen((dense[23, e] >= 0.0).astype(F32))


def mixed(side, mine, on):
    out = []
    for m in range(2):
        for n in range(2):
            v = sum(side[17 + 3 * m + a] * mine[17 + 3 * n + a] for a in range(3))
            out.append(on - v if m == n else -v)
    return out


def pack_kernel(jc, jp, rs, damp, cl, slot, first, second, dense, found_ref, fields, kept):
    step = pl.program_id(0)

    @pl.when(step == 0)
    def _():
        points_part(jc, jp, rs, damp, cl, slot, dense, found_ref, fields)

    for part in range(PAIRS):
        pack_pair(step * PAIRS + part, part, first, second, dense, found_ref, kept)


def pack_pair(pair, part, first, second, dense, found_ref, kept):
    for ec in range(2):
        found = lanes_of(found_ref[ec, pl.ds(pair, 1), :], NROW)
        pick = jnp.minimum(found, PTS - 1)
        side = [
            [jnp.take_along_axis(dense[f, e], pick, axis=1) for f in range(24)] for e in range(2)
        ]
        for f in range(29):
            if f < 24:
                kept[2 * part + ec, f] = side[ec][f]
            else:
                kept[2 * part + ec, f] = jnp.take_along_axis(dense[f, ec], pick, axis=1)
        mine = [lanes_of(kept[2 * part + ec, f, pl.ds(pair, 1), :], NROW) for f in range(29)]
        middle = []
        for e in range(2):
            same = jnp.where(iota((NROW, PTS), 0) == pair, float(e == ec), 0.0)
            middle.append(mixed(side[e], mine, same))
        slot = jnp.where(found < PTS, mine[23], -1.0)
        extra = [side[0][16], mine[16]] + middle[0] + [side[0][23], slot]
        store(first, 2 * part + ec, side[0][0:16] + mine[0:16], extra)
        rows = side[1][0:17] + [side[1][23]] + mine[24:29] + middle[1][0:1]
        store(second, 2 * part + ec, rows, middle[1][1:4])


def store(out_ref, at, rows, extra):
    lane = iota((NROW, PTS), 1)
    zero = jnp.zeros((NROW, PTS), F32)
    sent = len(rows)
    flat = out_ref.reshape(NROW * 2 * PAIRS * sent, PTS)
    for r, row in enumerate(rows):
        v, x = r // 8, r % 8
        rest = pltpu.roll(extra[x], 96 - 32 * v, 1) if v < 3 and x < len(extra) else zero
        value = jnp.where(lane < CAP, row, rest)
        flat[pl.ds(sent * at + r, NROW, stride=2 * PAIRS * sent), :] = value


def pack(*args):
    return pl.pallas_call(
        pack_kernel,
        grid=(NROW // PAIRS,),
        in_specs=[whole(*a.shape) for a in args],
        out_specs=[
            pl.BlockSpec((NROW, 2 * PAIRS, n, PTS), lambda g: (0, g, 0, 0)) for n in (FIRST, SECOND)
        ],
        out_shape=[jax.ShapeDtypeStruct((NROW, NCL, n, PTS), F32) for n in (FIRST, SECOND)],
        scratch_shapes=[
            pltpu.VMEM((29, 2, NROW, PTS), F32),
            pltpu.VMEM((2, NROW, PTS), jnp.int32),
            pltpu.VMEM((29, KOBS, PTS), F32),
            pltpu.VMEM((2 * PAIRS, 29, NROW, PTS), F32),
        ],
        name="pack",
        **settings(8, 60),
    )(*args)


def exchange(value):
    return lax.all_to_all(value, AXES, split_axis=0, concat_axis=0, tiled=True)


FIRST, SECOND = 32, 24


def lay(in_ref, rows_ref):
    lane = iota((8, PTS), 1)
    full = iota(rows_ref.shape[0:1] + (PTS,), 1)
    for quarter in range(SRC // 4):
        pieces = []
        for s in range(4):
            block = in_ref[quarter * 4 + s]
            part = [block[8 * v : 8 * v + 8] for v in range(3)]
            part = [pltpu.roll(p, 32 + 32 * v, 1) for v, p in enumerate(part)]
            rest = jnp.where(lane < 32, part[0], jnp.where(lane < 64, part[1], part[2]))
            pieces.append(jnp.concatenate([block, rest], axis=0))
        r1, r2 = pltpu.roll(pieces[1], 96, 1), pltpu.roll(pieces[2], 64, 1)
        r3 = pltpu.roll(pieces[3], 32, 1)
        base = quarter * 384
        rows_ref[:, base : base + 128] = jnp.where(full < 96, pieces[0], r1)
        rows_ref[:, base + 128 : base + 256] = jnp.where(full < 64, r1, r2)
        rows_ref[:, base + 256 : base + 384] = jnp.where(full < 32, r2, r3)


def jacobian(rows_ref, at, last):
    first = iota((8, LANES), 0) == 0
    a1 = jnp.where(first, 0.0, rows_ref[at + 8 : at + 16])
    return rows_ref[at : at + 8], a1, rows_ref[at + 8 : at + 9], rows_ref[last : last + 1]


def side_of(e, one, two):
    if e:
        return jacobian(two, 0, 16), [two[23 + n : 24 + n] for n in range(4)], two[17:18]
    return jacobian(one, 0, 32), [one[34 + n : 35 + n] for n in range(4)], one[38:39]


def cg_kernel(flag_ref, one, in_ref, damp_ref, two, out_ref, keep1, keep2, hits, sums, image):
    step = pl.program_id(0)
    steps = pl.num_programs(0)

    @pl.when(step == 0)
    def _():
        sums[...] = jnp.zeros_like(sums)

    lay(in_ref, two)
    a0, a1, l0, l1 = jacobian(one, 16, 33)
    q0, q1 = two[18:19], two[19:20]
    m0, m1, m2 = two[20:21], two[21:22], two[22:23]
    terms = [
        a0 * lanes_of(q0, 8) + a1 * lanes_of(q1, 8),
        a0 * a0 * lanes_of(m0, 8) + a0 * a1 * lanes_of(m1, 8) + a1 * a1 * lanes_of(m2, 8),
        l0 * q0 + l1 * q1,
        l0 * l0 * m0 + l0 * l1 * m1 + l1 * l1 * m2,
        jnp.zeros((14, LANES), F32),
    ]
    hit = hot(one[39:40].astype(jnp.int32), 128)
    hits[step] = hit
    keep1[step] = one[...]
    keep2[step] = two[...]
    sums[...] += lax.dot_general(
        three(jnp.concatenate(terms, axis=0)), hit, NT, preferred_element_type=F32
    )

    @pl.when(step == steps - 1)
    def _():
        damp = damp_ref[...]
        total = sums[0:24] + sums[32:56] + sums[64:88] + damp
        sums[0:24] = total
        x8, x9 = total[0:8] / total[8:16], total[16:17] / total[17:18]
        x = three(jnp.concatenate([x8, x9, jnp.zeros((7, 128), F32)], axis=0))
        image[...] = jnp.zeros_like(image)

        for at in range(NDEV // SRC):
            rows1, rows2 = keep1.at[at], keep2.at[at]
            got = jnp.dot(x, hits[at], preferred_element_type=F32)
            got = got[0:16] + got[16:32] + got[32:48]
            a0, a1, l0, l1 = jacobian(rows1, 16, 33)
            v0 = jnp.sum(a0 * got[0:8], axis=0, keepdims=True) + l0 * got[8:9]
            v1 = jnp.sum(a1 * got[0:8], axis=0, keepdims=True) + l1 * got[8:9]
            for e in range(2):
                (a0, a1, l0, l1), m, slot = side_of(e, rows1, rows2)
                z0, z1 = m[0] * v0 + m[1] * v1, m[2] * v0 + m[3] * v1
                out8 = a0 * lanes_of(z0, 8) + a1 * lanes_of(z1, 8)
                terms = [out8, l0 * z0 + l1 * z1, jnp.zeros((7, LANES), F32)]
                slot = slot.astype(jnp.int32)
                hit = hot(jnp.where(slot >= 0, slot + CAM * e, -1), 128)
                image[...] += lax.dot_general(
                    three(jnp.concatenate(terms, axis=0)), hit, NT, preferred_element_type=F32
                )

        y = image[0:16] + image[16:32] + image[32:48]
        own = iota((16, 128), 1) < CAM
        extra = jnp.concatenate([damp[8:16] * x8, damp[17:18] * x9, jnp.zeros((7, 128), F32)], axis=0)
        extra = jnp.where(own, extra, 0.0)
        y += jnp.where(flag_ref[0] == 1, extra, 0.0)
        y += jnp.where(flag_ref[1] == 1, pltpu.roll(extra, CAM, 1), 0.0)
        part = sums[pl.ds(3 * flag_ref[2], 3), :]
        block = jnp.concatenate([y[0:9], part, jnp.zeros((4, 128), F32)], axis=0)
        out_ref[...] = jnp.broadcast_to(block[None], (NDEV, 16, 128))

def cg_part(flags, one, incoming, damp):
    steps = NDEV // SRC
    return pl.pallas_call(
        cg_kernel,
        grid=(steps,),
        in_specs=[
            pl.BlockSpec(memory_space=pltpu.SMEM),
            pl.BlockSpec(((FIRST + 8), LANES), lambda s: (0, s)),
            pl.BlockSpec((SRC, SECOND, PTS), lambda s: (s, 0, 0)),
            whole(24, 128),
        ],
        out_specs=[
            pl.BlockSpec(((SECOND + 8), LANES), lambda s: (0, s)),
            whole(NDEV, 16, 128),
        ],
        out_shape=[
            jax.ShapeDtypeStruct(((SECOND + 8), steps * LANES), F32),
            jax.ShapeDtypeStruct((NDEV, 16, 128), F32),
        ],
        scratch_shapes=[
            pltpu.VMEM((steps, (FIRST + 8), LANES), F32),
            pltpu.VMEM((steps, (SECOND + 8), LANES), F32),
            pltpu.VMEM((steps, 128, LANES), BF),
            pltpu.VMEM((96, 128), F32),
            pltpu.VMEM((48, 128), F32),
        ],
        name="cg",
        **settings(6, 60),
    )(flags, one, incoming, damp)


SCALE = 2048.0


def add_products(e, one, two, prod, acc):
    def split(value):
        high = value.astype(BF).astype(F32)
        return high, value - high

    (a0, a1, last0, last1), middle, slot_a = side_of(e, one, two)
    cam0, cam1, cam_last0, cam_last1 = jacobian(one, 16, 33)
    t, t_last = [], []
    for m in range(2):
        m0, m1 = middle[2 * m] * SCALE, middle[2 * m + 1] * SCALE
        t.append(lanes_of(m0, 8) * cam0 + lanes_of(m1, 8) * cam1)
        t_last.append(m0 * cam_last0 + m1 * cam_last1)
    for j in range(9):
        t0 = t[0][j : j + 1] if j < 8 else t_last[0]
        t1 = t[1][j : j + 1] if j < 8 else t_last[1]
        high, low = split(a0 * lanes_of(t0, 8) + a1 * lanes_of(t1, 8))
        prod[0, j, 0:8] = high
        prod[1, j, 0:8] = low
        high, low = split(last0 * t0 + last1 * t1)
        prod[0, j, 8:9] = high
        prod[1, j, 8:9] = low
    slot_a, slot_c = slot_a.astype(jnp.int32), one[39:40].astype(jnp.int32)
    both = jnp.minimum(slot_a, slot_c) >= 0
    code = jnp.where(both, (slot_a >> 4) * CAM + slot_c, -1)
    onehot = hot(code, 256)
    mask = hot(slot_a & 15, 16)
    n = GROUP * 144
    onehot8 = onehot.astype(F8)
    for g in range(9 // GROUP):
        parts = [[], []]
        for h in range(2):
            for j in range(g * GROUP, (g + 1) * GROUP):
                for i in range(9):
                    parts[h].append(lanes_of(prod[h, j, i : i + 1], 16).astype(BF) * mask)
        high = jnp.concatenate(parts[0], axis=0)
        low = jnp.concatenate(parts[1], axis=0).astype(F8)
        got = lax.dot_general(high, onehot, NT, preferred_element_type=F32)
        rest = lax.dot_general(low, onehot8, NT, preferred_element_type=F32)
        acc[g * n : (g + 1) * n, :] += got + rest


def assemble(read, flag, damp_ref, out_ref, stage, wide_ref):
    source = iota((640, 640), 0)
    place = iota((640, 640), 1) == 9 * (source % CAM) + source // CAM
    place = (place & (source < TILE)).astype(F32).astype(BF)
    lane = iota((144, PTS), 1)
    for u in range(4):
        base = (u // 2) * 128
        tiles = []
        for jj in range(5):
            even = read(2 * jj, base)
            if u % 2:
                even = pltpu.roll(even, 64, 1)
            if jj < 4:
                odd = read(2 * jj + 1, base)
                if u % 2 == 0:
                    odd = pltpu.roll(odd, 64, 1)
                even = jnp.where(lane < CAM, even, odd)
            tiles.append(even)
        full = jnp.concatenate(tiles, axis=1) * (1.0 / SCALE)
        high = full.astype(BF)
        wide_ref[144 * u : 144 * u + 144] = high
        wide_ref[TILE + 144 * u : TILE + 144 * u + 144] = (full - high.astype(F32)).astype(BF)
    got = jnp.dot(wide_ref[...], place, preferred_element_type=F32)
    got = got[:TILE] + got[TILE:]
    for u in range(4):
        for tile in range(5):
            for i in range(9):
                at = 144 * u + 16 * i
                piece = got[at : at + 16, 128 * tile : 128 * tile + 128]
                stage[pl.ds(TILE * tile + 144 * u + i, 16, stride=9), :] = piece
    for tile in range(5):
        wide = min(128, TILE - 128 * tile)
        block = stage[TILE * tile : TILE * tile + TILE, 0:wide]
        out_ref[0, :, 128 * tile : 128 * tile + wide] = block

    @pl.when(flag == 1)
    def _():
        same = iota((TILE, TILE), 0) == iota((TILE, TILE), 1)
        out_ref[0] += jnp.where(same, jnp.broadcast_to(damp_ref[...], (TILE, TILE)), 0.0)


def spread_kernel(e, flag_ref, damp_ref, *refs):
    if e:
        one, two, out_ref, token, prod, acc, stage, wide_ref = refs[0], refs[1], *refs[4:]
    else:
        in_ref, out_ref, one, prod, acc, stage, wide_ref = refs
    step = pl.program_id(0)

    @pl.when(step == 0)
    def _():
        acc[...] = jnp.zeros_like(acc)

    if e:
        add_products(1, one, two, prod, acc)
    else:
        lay(in_ref, one)
        add_products(0, one, None, prod, acc)

    @pl.when(step == pl.num_programs(0) - 1)
    def _():
        def read(j, base):
            return acc[144 * j : 144 * j + 144, base : base + 128]

        assemble(read, flag_ref[e], damp_ref, out_ref, stage, wide_ref)
        if e:
            token[...] = jnp.zeros_like(token)


def spread(e, flags, damp, args):
    steps = NDEV // SRC
    in_specs = [pl.BlockSpec(memory_space=pltpu.SMEM), whole(1, TILE)]
    tile_spec = pl.BlockSpec((1, TILE, TILE), lambda s: (e, 0, 0))
    tile_shape = jax.ShapeDtypeStruct((2, TILE, TILE), F32)
    if e:
        in_specs += [
            pl.BlockSpec(((FIRST + 8), LANES), lambda s: (0, s)),
            pl.BlockSpec(((SECOND + 8), LANES), lambda s: (0, s)),
            ANY,
            ANY,
        ]
        out_specs = [tile_spec, whole(8, 128)]
        out_shape = [tile_shape, jax.ShapeDtypeStruct((8, 128), F32)]
    else:
        in_specs.append(pl.BlockSpec((SRC, FIRST, PTS), lambda s: (s, 0, 0)))
        out_specs = [tile_spec, pl.BlockSpec(((FIRST + 8), LANES), lambda s: (0, s))]
        out_shape = [tile_shape, jax.ShapeDtypeStruct(((FIRST + 8), steps * LANES), F32)]
    return pl.pallas_call(
        functools.partial(spread_kernel, e),
        grid=(steps,),
        in_specs=in_specs,
        out_specs=out_specs,
        out_shape=out_shape,
        scratch_shapes=[
            pltpu.VMEM((2, 9, 16, LANES), F32),
            pltpu.VMEM((1296, 256), F32),
            pltpu.VMEM((5 * TILE, 128), F32),
            pltpu.VMEM((2 * TILE, 640), BF),
        ],
        input_output_aliases={4: 0} if e else {},
        name="spread",
        **settings(20, 60),
    )(flags, damp, *args)


def finish_kernel(in_ref, behind, step_ref, res_ref, dir_ref):
    pieces = []
    for r in range(NROW):
        pieces.append(jnp.sum(in_ref[NCL * r : NCL * r + NCL], axis=0))
    lane = iota((16, 128), 1)
    image = jnp.concatenate([jnp.where(iota((16, 128), 0) < 9, p, 0.0) for p in pieces], axis=1)
    both = []
    for c in range(NCL):
        rows = jnp.concatenate([in_ref[NCL * r + c, 9:12, :] for r in range(6)], axis=0)
        both.append(rows)
    wide = iota((18, 128), 1)
    both = [
        jnp.where(wide < CAM, both[2 * g], pltpu.roll(both[2 * g + 1], CAM, 1))
        for g in range(NCL // 2)
    ]
    both = jnp.concatenate(both, axis=1)
    pad = jnp.zeros((7, NCL * CAM), F32)
    rhs = jnp.concatenate([both[0:8], both[16:17], pad], axis=0)
    diag = jnp.concatenate([both[8:16], both[17:18], pad + 1.0], axis=0)
    start = rhs / diag
    rz = jnp.sum(rhs * start)
    alpha = rz / jnp.sum(start * image)
    residual = rhs - alpha * image
    second = residual / diag
    beta = jnp.sum(residual * second) / rz
    values = (alpha * start, residual, second + beta * start)
    for r in range(9):
        at = 128 * r + lane
        camera = at // 9
        keep = at - 9 * camera == iota((16, 128), 0)
        camera = camera[0:8]
        for value, ref in zip(values, (step_ref, res_ref, dir_ref)):
            for g in range(NCL // 2):
                part = value[:, 128 * g : 128 * g + 128]
                top = jnp.take_along_axis(part[0:8], camera, axis=1)
                low = jnp.take_along_axis(part[8:16], camera, axis=1)
                found = jnp.where(keep, jnp.concatenate([top, low], axis=0), 0.0)
                ref[9 * g + r : 9 * g + r + 1, :] = jnp.sum(found, axis=0, keepdims=True)


def finish(incoming, behind):
    return pl.pallas_call(
        finish_kernel,
        grid=(1,),
        in_specs=[whole(NDEV, 16, 128), ANY],
        out_specs=[whole(72, 128)] * 3,
        out_shape=[jax.ShapeDtypeStruct((72, 128), F32)] * 3,
        name="finish",
        **settings(3, 60),
    )(incoming, behind)


def shards(jac_cam, jac_pt, resid, point_damp, cam_damp, obs_cluster, obs_slot):
    my_row = lax.axis_index("row")
    my_col = lax.axis_index("col")
    flags = (2 * my_row + jnp.arange(2) == my_col).astype(jnp.int32)
    flags = jnp.concatenate([flags, my_row[None].astype(jnp.int32)])
    damp = jnp.pad(cam_damp.reshape(CAM, 9).T, ((0, 0), (0, 128 - CAM)), constant_values=1.0)
    zeros = jnp.zeros((8, 128), F32)
    damp = jnp.concatenate([zeros, damp[0:8], zeros[0:1], damp[8:9], zeros[0:6]], axis=0)
    first, second = pack(
        jac_cam.transpose(1, 0, 2), jac_pt.transpose(1, 0, 2), resid, point_damp, obs_cluster.T,
        obs_slot,
    )
    first = exchange(first.reshape(NDEV, FIRST, PTS))
    second = exchange(second.reshape(NDEV, SECOND, PTS))
    tiles, one = spread(0, flags, cam_damp, (first,))
    two, share = cg_part(flags, one, second, damp)
    shares = exchange(share)
    tiles, token = spread(1, flags, cam_damp, (one, two, tiles, share))
    step, residual, direction = finish(shares, token)
    return (tiles[:, None], step.reshape(-1), residual.reshape(-1), direction.reshape(-1))


def solution(mesh):
    placed = (
        P(None, None, AXES),
        P(None, None, AXES),
        P(None, None, AXES),
        P(None, AXES),
        P("col", None),
        P(AXES, None),
        P(None, AXES),
    )
    return jax.shard_map(
        shards,
        mesh=mesh,
        in_specs=placed,
        out_specs=(P("row", "col", None, None), P(), P(), P()),
        check_vma=False,
    )
```

```python
import functools

import jax
import jax.numpy as jnp
from jax import lax
from jax.experimental import pallas as pl
from jax.experimental.pallas import tpu as pltpu
from jax.sharding import PartitionSpec as P

KOBS = 8
NCL = 16
CAP = 96
CAM = 64
TILE = 576
NROW = 8
NDEV = 128
PTS = 128
AXES = ("row", "col")
BF = jnp.bfloat16
F8 = jnp.float8_e4m3fn
F32 = jnp.float32
NT = (((1,), (1,)), ((), ()))
MIB = 1 << 20
SRC = 32
PAIRS = 2
LANES = SRC * CAP
GROUP = 3
ANY = pl.BlockSpec(memory_space=pl.ANY)


def iota(shape, dim):
    return lax.broadcasted_iota(jnp.int32, shape, dim)


def whole(*shape):
    return pl.BlockSpec(shape, lambda *_: (0,) * len(shape))


def settings(micros, mib):
    return dict(
        compiler_params=pltpu.CompilerParams(vmem_limit_bytes=mib * MIB),
        cost_estimate=pl.CostEstimate(
            flops=micros * 10**9, bytes_accessed=10**6, transcendentals=0
        ),
    )


def lanes_of(row, n):
    return jnp.broadcast_to(row, (n, row.shape[1]))


def whitened(jp, rs, damp):
    def inner(a, b):
        return jnp.sum(jp[0][a] * jp[0][b] + jp[1][a] * jp[1][b], axis=0, keepdims=True)

    laa = jnp.sqrt(inner(0, 0) + damp[0:1])
    lba = inner(1, 0) / laa
    lca = inner(2, 0) / laa
    lbb = jnp.sqrt(inner(1, 1) + damp[1:2] - lba * lba)
    lcb = (inner(2, 1) - lca * lba) / lbb
    lcc = jnp.sqrt(inner(2, 2) + damp[2:3] - lca * lca - lcb * lcb)

    def solve(a, b, c):
        x = a / laa
        y = (b - lba * x) / lbb
        return [x, y, (c - lca * x - lcb * y) / lcc]

    u = [solve(*jp[m]) for m in range(2)]
    grad = [
        jnp.sum(jp[0][a] * rs[0] + jp[1][a] * rs[1], axis=0, keepdims=True) for a in range(3)
    ]
    w = solve(*grad)
    q = [u[m][0] * w[0] + u[m][1] * w[1] + u[m][2] * w[2] - rs[m] for m in range(2)]
    return u, q


def hot(code, n):
    codes = lanes_of(code.astype(F32), n).astype(BF)
    ids = iota((n, code.shape[1]), 0).astype(F32).astype(BF)
    return jnp.where(codes == ids, jnp.ones((), BF), jnp.zeros((), BF))


def halves(value):
    high = value.astype(BF)
    return jnp.concatenate([high, (value - high.astype(F32)).astype(BF)], axis=0)


def chosen(named):
    upto = (iota((PTS, PTS), 0) <= iota((PTS, PTS), 1)).astype(F32).astype(BF)
    counts = jnp.dot(named.astype(BF), upto, preferred_element_type=F32)
    lane = iota(named.shape, 1)
    at = jnp.zeros(named.shape, jnp.int32)
    for jump in (64, 32, 16, 8, 4, 2, 1):
        seen = jnp.take_along_axis(counts, at + (jump - 1), axis=1)
        at = jnp.where(seen <= lane.astype(F32), at + jump, at)
    return jnp.where(lane.astype(F32) < counts[:, PTS - 1 : PTS], at, PTS)


def points_part(jc, jp, rs, damp, cl_ref, slot_ref, dense, found_ref, fields):
    cl, slot = cl_ref[...], slot_ref[...]
    u, q = whitened(
        [[jp[m * 3 + a] for a in range(3)] for m in range(2)],
        [rs[:, m, :] for m in range(2)],
        damp[...],
    )
    j0, j1 = jc[0], jc[9]
    top = jnp.maximum(jnp.abs(j0), jnp.abs(j1))
    some = top > 0.0
    safe = jnp.where(some, top, 1.0)
    x, y = j0 / safe, j1 / safe
    length = jnp.where(some, jnp.sqrt(x * x + y * y), 1.0)
    cs = jnp.where(some, x / length, 1.0)
    sn = jnp.where(some, y / length, 0.0)
    for i in range(9):
        a, b = jc[i], jc[9 + i]
        fields[i] = cs * a + sn * b
        if i:
            fields[8 + i] = cs * b - sn * a
    turned = [[], []]
    for a in range(3):
        turned[0].append(cs * u[0][a] + sn * u[1][a])
        turned[1].append(cs * u[1][a] - sn * u[0][a])
        fields[17 + a] = turned[0][a]
        fields[20 + a] = turned[1][a]
    fields[23] = slot.astype(F32)
    fields[24] = cs * q[0] + sn * q[1]
    fields[25] = cs * q[1] - sn * q[0]
    fields[26] = 1.0 - sum(v * v for v in turned[0])
    fields[27] = -2.0 * sum(v * w for v, w in zip(*turned))
    fields[28] = 1.0 - sum(v * v for v in turned[1])
    for e in range(2):
        ids = 2 * iota((NROW, PTS), 0) + e
        hits = [lanes_of(cl[k : k + 1], NROW) == ids for k in range(KOBS)]
        for f in range(29):
            value = jnp.full((NROW, PTS), -1.0 if f == 23 else 0.0, F32)
            for k in range(KOBS):
                value = jnp.where(hits[k], lanes_of(fields[f, k : k + 1, :], NROW), value)
            dense[f, e] = value
        found_ref[e] = chosen((dense[23, e] >= 0.0).astype(F32))


def mixed(side, mine, on):
    out = []
    for m in range(2):
        for n in range(2):
            v = sum(side[17 + 3 * m + a] * mine[17 + 3 * n + a] for a in range(3))
            out.append(on - v if m == n else -v)
    return out


def picked(dense, found_ref, pair, ec):
    found = lanes_of(found_ref[ec, pl.ds(pair, 1), :], NROW)
    pick = jnp.minimum(found, PTS - 1)
    same = [jnp.where(iota((NROW, PTS), 0) == pair, float(e == ec), 0.0) for e in range(2)]
    return found, same, lambda f, e: jnp.take_along_axis(dense[f, e], pick, axis=1)


def in_lists(rows, extra, slots):
    lane = iota((NROW, PTS), 1)
    rest = [jnp.zeros((NROW, PTS), F32)] * len(rows)
    for value, places in zip(extra, slots):
        for v, r in enumerate(places):
            rest[r] = pltpu.roll(value, 96 - 32 * v, 1)
    return [jnp.where(lane < CAP, a, b) for a, b in zip(rows, rest)]


FIRST_SLOTS = [(x, 8 + x, 16 + x) for x in range(8)] + [(24, 25, 26)]
SECOND_SLOTS = [(x, 6 + x, 12 + x) for x in range(6)]


def pack_first_kernel(jc, jp, rs, damp, cl, slot, out_ref, dense, found_ref, fields, kept):
    step = pl.program_id(0)

    @pl.when(step == 0)
    def _():
        points_part(jc, jp, rs, damp, cl, slot, dense, found_ref, fields)

    for part in range(PAIRS):
        pair = step * PAIRS + part
        for ec in range(2):
            found, same, take = picked(dense, found_ref, pair, ec)
            side = [take(f, 0) for f in range(24)]
            for f in range(24):
                kept[2 * part + ec, f] = take(f, 1) if ec else side[f]
            mine = [lanes_of(kept[2 * part + ec, f, pl.ds(pair, 1), :], NROW) for f in range(24)]
            list_slot = jnp.where(found < PTS, mine[23], -1.0)
            extra = [side[16], mine[16]] + mixed(side, mine, same[0]) + [side[23], list_slot]
            extra.append(take(23, 1))
            values = in_lists(side[0:16] + mine[0:16], extra, FIRST_SLOTS)
            for r in range(0, FIRST, 8):
                block = jnp.swapaxes(jnp.stack(values[r : r + 8], axis=0), 0, 1)
                out_ref[:, 2 * part + ec, r : r + 8, :] = block


def pack_second_kernel(dense, found_ref, out_ref, kept):
    step = pl.program_id(0)
    for part in range(PAIRS):
        pair = step * PAIRS + part
        for ec in range(2):
            _, same, take = picked(dense, found_ref, pair, ec)
            side = [take(f, 1) for f in range(23)]
            for f in range(17, 29):
                if f != 23:
                    kept[2 * part + ec, f] = take(f, ec)
            mine = {
                f: lanes_of(kept[2 * part + ec, f, pl.ds(pair, 1), :], NROW)
                for f in range(17, 29)
                if f != 23
            }
            rows = side[0:17] + [mine[24], mine[25], mine[26]]
            extra = [mine[27], mine[28]] + mixed(side, mine, same[1])
            values = in_lists(rows, extra, SECOND_SLOTS)
            values += values[0:4]
            for r in range(0, SECOND, 8):
                block = jnp.swapaxes(jnp.stack(values[r : r + 8], axis=0), 0, 1)
                out_ref[:, 2 * part + ec, r // 4] = block[:, 0:4]
                if r + 4 < SECOND:
                    out_ref[:, 2 * part + ec, r // 4 + 1] = block[:, 4:8]


def pack_first(*args):
    return pl.pallas_call(
        pack_first_kernel,
        grid=(NROW // PAIRS,),
        in_specs=[whole(*a.shape) for a in args],
        out_specs=[
            pl.BlockSpec((NROW, 2 * PAIRS, FIRST, PTS), lambda g: (0, g, 0, 0)),
            whole(29, 2, NROW, PTS),
            whole(2, NROW, PTS),
        ],
        out_shape=[
            jax.ShapeDtypeStruct((NROW, NCL, FIRST, PTS), F32),
            jax.ShapeDtypeStruct((29, 2, NROW, PTS), F32),
            jax.ShapeDtypeStruct((2, NROW, PTS), jnp.int32),
        ],
        scratch_shapes=[
            pltpu.VMEM((29, KOBS, PTS), F32),
            pltpu.VMEM((2 * PAIRS, 24, NROW, PTS), F32),
        ],
        name="pack_first",
        **settings(5, 60),
    )(*args)


def pack_second(dense, found):
    return pl.pallas_call(
        pack_second_kernel,
        grid=(NROW // PAIRS,),
        in_specs=[whole(29, 2, NROW, PTS), whole(2, NROW, PTS)],
        out_specs=pl.BlockSpec(
            (NROW, 2 * PAIRS, SECOND // 4, 4, PTS), lambda g: (0, g, 0, 0, 0)
        ),
        out_shape=jax.ShapeDtypeStruct((NROW, NCL, SECOND // 4, 4, PTS), F32),
        scratch_shapes=[pltpu.VMEM((2 * PAIRS, 29, NROW, PTS), F32)],
        name="pack_second",
        **settings(5, 60),
    )(dense, found)


def exchange(value):
    return lax.all_to_all(value, AXES, split_axis=0, concat_axis=0, tiled=True)


FIRST, FIRST_ROWS = 32, 41
SECOND, SECOND_ROWS = 20, 26


def joined(a, b, c):
    lane = iota(a.shape, 1)
    a, b, c = pltpu.roll(a, 32, 1), pltpu.roll(b, 64, 1), pltpu.roll(c, 96, 1)
    return jnp.where(lane < 32, a, jnp.where(lane < 64, b, c))


def lay(in_ref, rows_ref):
    full = iota(rows_ref.shape[0:1] + (PTS,), 1)
    for quarter in range(SRC // 4):
        pieces = []
        for s in range(quarter * 4, quarter * 4 + 4):
            if len(in_ref.shape) == 3:
                block = in_ref[s]
                rest = [joined(block[0:8], block[8:16], block[16:24])]
                rest.append(joined(block[24:25], block[25:26], block[26:27]))
            else:
                block = jnp.concatenate([in_ref[s, k] for k in range(SECOND // 4)], axis=0)
                rest = [joined(block[0:6], block[6:12], block[12:18])]
            pieces.append(jnp.concatenate([block] + rest, axis=0))
        r1, r2 = pltpu.roll(pieces[1], 96, 1), pltpu.roll(pieces[2], 64, 1)
        r3 = pltpu.roll(pieces[3], 32, 1)
        base = quarter * 384
        rows_ref[:, base : base + 128] = jnp.where(full < 96, pieces[0], r1)
        rows_ref[:, base + 128 : base + 256] = jnp.where(full < 64, r1, r2)
        rows_ref[:, base + 256 : base + 384] = jnp.where(full < 32, r2, r3)


def jacobian(rows_ref, at, last):
    first = iota((8, LANES), 0) == 0
    a1 = jnp.where(first, 0.0, rows_ref[at + 8 : at + 16])
    return rows_ref[at : at + 8], a1, rows_ref[at + 8 : at + 9], rows_ref[last : last + 1]


def side_of(e, one, two):
    if e:
        return jacobian(two, 0, 16), [two[22 + n : 23 + n] for n in range(4)], one[40:41]
    return jacobian(one, 0, 32), [one[34 + n : 35 + n] for n in range(4)], one[38:39]


def cg_kernel(flag_ref, one, in_ref, damp_ref, two, out_ref, keep1, keep2, hits, sums, image, kept):
    step = pl.program_id(0)
    steps = pl.num_programs(0)

    @pl.when(step == 0)
    def _():
        sums[...] = jnp.zeros_like(sums)

    lay(in_ref, two)
    a0, a1, l0, l1 = jacobian(one, 16, 33)
    q0, q1 = two[17:18], two[18:19]
    m0, m1, m2 = two[19:20], two[20:21], two[21:22]
    terms = [
        a0 * lanes_of(q0, 8) + a1 * lanes_of(q1, 8),
        a0 * a0 * lanes_of(m0, 8) + a0 * a1 * lanes_of(m1, 8) + a1 * a1 * lanes_of(m2, 8),
        l0 * q0 + l1 * q1,
        l0 * l0 * m0 + l0 * l1 * m1 + l1 * l1 * m2,
        jnp.zeros((14, LANES), F32),
    ]
    hit = hot(one[39:40].astype(jnp.int32), CAM)
    hits[step] = hit
    keep1[step] = one[...]
    keep2[step] = two[...]
    sums[...] += lax.dot_general(
        halves(jnp.concatenate(terms, axis=0)), hit, NT, preferred_element_type=F32
    )

    @pl.when(step == steps - 1)
    def _():
        damp = damp_ref[...]
        total = sums[0:24] + sums[32:56] + damp
        kept[...] = jnp.concatenate([total, jnp.zeros_like(total)], axis=1)
        x8, x9 = total[0:8] / total[8:16], total[16:17] / total[17:18]
        x = halves(jnp.concatenate([x8, x9, jnp.zeros((7, CAM), F32)], axis=0))
        image[...] = jnp.zeros_like(image)

        for at in range(NDEV // SRC):
            rows1, rows2 = keep1.at[at], keep2.at[at]
            got = jnp.dot(x, hits[at], preferred_element_type=F32)
            got = got[0:16] + got[16:32]
            a0, a1, l0, l1 = jacobian(rows1, 16, 33)
            v0 = jnp.sum(a0 * got[0:8], axis=0, keepdims=True) + l0 * got[8:9]
            v1 = jnp.sum(a1 * got[0:8], axis=0, keepdims=True) + l1 * got[8:9]
            for e in range(2):
                (a0, a1, l0, l1), m, slot = side_of(e, rows1, rows2)
                z0, z1 = m[0] * v0 + m[1] * v1, m[2] * v0 + m[3] * v1
                out8 = a0 * lanes_of(z0, 8) + a1 * lanes_of(z1, 8)
                terms = [out8, l0 * z0 + l1 * z1, jnp.zeros((7, LANES), F32)]
                image[e] += lax.dot_general(
                    halves(jnp.concatenate(terms, axis=0)),
                    hot(slot.astype(jnp.int32), CAM),
                    NT,
                    preferred_element_type=F32,
                )

        extra = jnp.concatenate([damp[8:16] * x8, damp[17:18] * x9, jnp.zeros((7, CAM), F32)], axis=0)
        y = [
            image[e, 0:16] + image[e, 16:32] + jnp.where(flag_ref[e] == 1, extra, 0.0)
            for e in range(2)
        ]
        y = jnp.concatenate(y, axis=1)
        part = kept[pl.ds(3 * flag_ref[2], 3), :]
        block = jnp.concatenate([y[0:9], part, jnp.zeros((4, 128), F32)], axis=0)
        out_ref[...] = jnp.broadcast_to(block[None], (NDEV, 16, 128))

def cg_part(flags, one, incoming, damp):
    steps = NDEV // SRC
    return pl.pallas_call(
        cg_kernel,
        grid=(steps,),
        in_specs=[
            pl.BlockSpec(memory_space=pltpu.SMEM),
            pl.BlockSpec((FIRST_ROWS, LANES), lambda s: (0, s)),
            pl.BlockSpec((SRC, SECOND // 4, 4, PTS), lambda s: (s, 0, 0, 0)),
            whole(24, CAM),
        ],
        out_specs=[
            pl.BlockSpec((SECOND_ROWS, LANES), lambda s: (0, s)),
            whole(NDEV, 16, 128),
        ],
        out_shape=[
            jax.ShapeDtypeStruct((SECOND_ROWS, steps * LANES), F32),
            jax.ShapeDtypeStruct((NDEV, 16, 128), F32),
        ],
        scratch_shapes=[
            pltpu.VMEM((steps, FIRST_ROWS, LANES), F32),
            pltpu.VMEM((steps, SECOND_ROWS, LANES), F32),
            pltpu.VMEM((steps, CAM, LANES), BF),
            pltpu.VMEM((64, CAM), F32),
            pltpu.VMEM((2, 32, CAM), F32),
            pltpu.VMEM((24, 128), F32),
        ],
        name="cg",
        **settings(6, 63),
    )(flags, one, incoming, damp)


SCALE = 2048.0


def add_products(e, one, two, prod, acc):
    def split(value):
        high = value.astype(BF).astype(F32)
        return high, value - high

    (a0, a1, last0, last1), middle, slot_a = side_of(e, one, two)
    cam0, cam1, cam_last0, cam_last1 = jacobian(one, 16, 33)
    t, t_last = [], []
    for m in range(2):
        m0, m1 = middle[2 * m] * SCALE, middle[2 * m + 1] * SCALE
        t.append(lanes_of(m0, 8) * cam0 + lanes_of(m1, 8) * cam1)
        t_last.append(m0 * cam_last0 + m1 * cam_last1)
    for j in range(9):
        t0 = t[0][j : j + 1] if j < 8 else t_last[0]
        t1 = t[1][j : j + 1] if j < 8 else t_last[1]
        high, low = split(a0 * lanes_of(t0, 8) + a1 * lanes_of(t1, 8))
        prod[0, j, 0:8] = high
        prod[1, j, 0:8] = low
        high, low = split(last0 * t0 + last1 * t1)
        prod[0, j, 8:9] = high
        prod[1, j, 8:9] = low
    slot_a, slot_c = slot_a.astype(jnp.int32), one[39:40].astype(jnp.int32)
    both = jnp.minimum(slot_a, slot_c) >= 0
    code = jnp.where(both, (slot_a >> 4) * CAM + slot_c, -1)
    onehot = hot(code, 256)
    mask = hot(slot_a & 15, 16)
    n = GROUP * 144
    onehot8 = onehot.astype(F8)
    for g in range(9 // GROUP):
        parts = [[], []]
        for h in range(2):
            for j in range(g * GROUP, (g + 1) * GROUP):
                for i in range(9):
                    parts[h].append(lanes_of(prod[h, j, i : i + 1], 16).astype(BF) * mask)
        high = jnp.concatenate(parts[0], axis=0)
        low = jnp.concatenate(parts[1], axis=0).astype(F8)
        got = lax.dot_general(high, onehot, NT, preferred_element_type=F32)
        rest = lax.dot_general(low, onehot8, NT, preferred_element_type=F32)
        acc[g * n : (g + 1) * n, :] += got + rest


def assemble(read, flag, damp_ref, out_ref, stage, wide_ref):
    source = iota((640, 640), 0)
    place = iota((640, 640), 1) == 9 * (source % CAM) + source // CAM
    place = (place & (source < TILE)).astype(F32).astype(BF)
    lane = iota((144, PTS), 1)
    for u in range(4):
        base = (u // 2) * 128
        tiles = []
        for jj in range(5):
            even = read(2 * jj, base)
            if u % 2:
                even = pltpu.roll(even, 64, 1)
            if jj < 4:
                odd = read(2 * jj + 1, base)
                if u % 2 == 0:
                    odd = pltpu.roll(odd, 64, 1)
                even = jnp.where(lane < CAM, even, odd)
            tiles.append(even)
        full = jnp.concatenate(tiles, axis=1) * (1.0 / SCALE)
        high = full.astype(BF)
        wide_ref[144 * u : 144 * u + 144] = high
        wide_ref[TILE + 144 * u : TILE + 144 * u + 144] = (full - high.astype(F32)).astype(BF)
    got = jnp.dot(wide_ref[...], place, preferred_element_type=F32)
    got = got[:TILE] + got[TILE:]
    for u in range(4):
        for tile in range(5):
            for i in range(9):
                at = 144 * u + 16 * i
                piece = got[at : at + 16, 128 * tile : 128 * tile + 128]
                stage[pl.ds(TILE * tile + 144 * u + i, 16, stride=9), :] = piece
    for tile in range(5):
        wide = min(128, TILE - 128 * tile)
        block = stage[TILE * tile : TILE * tile + TILE, 0:wide]
        out_ref[0, :, 128 * tile : 128 * tile + wide] = block

    @pl.when(flag == 1)
    def _():
        same = iota((TILE, TILE), 0) == iota((TILE, TILE), 1)
        out_ref[0] += jnp.where(same, jnp.broadcast_to(damp_ref[...], (TILE, TILE)), 0.0)


def spread_kernel(e, flag_ref, damp_ref, *refs):
    if e:
        one, two, out_ref, token, prod, acc, stage, wide_ref = refs[0], refs[1], *refs[4:]
    else:
        in_ref, out_ref, one, prod, acc, stage, wide_ref = refs
    step = pl.program_id(0)

    @pl.when(step == 0)
    def _():
        acc[...] = jnp.zeros_like(acc)

    if e:
        add_products(1, one, two, prod, acc)
    else:
        lay(in_ref, one)
        add_products(0, one, None, prod, acc)

    @pl.when(step == pl.num_programs(0) - 1)
    def _():
        def read(j, base):
            return acc[144 * j : 144 * j + 144, base : base + 128]

        assemble(read, flag_ref[e], damp_ref, out_ref, stage, wide_ref)
        if e:
            token[...] = jnp.zeros_like(token)


def spread(e, flags, damp, args):
    steps = NDEV // SRC
    in_specs = [pl.BlockSpec(memory_space=pltpu.SMEM), whole(1, TILE)]
    tile_spec = pl.BlockSpec((1, TILE, TILE), lambda s: (e, 0, 0))
    tile_shape = jax.ShapeDtypeStruct((2, TILE, TILE), F32)
    if e:
        in_specs += [
            pl.BlockSpec((FIRST_ROWS, LANES), lambda s: (0, s)),
            pl.BlockSpec((SECOND_ROWS, LANES), lambda s: (0, s)),
            ANY,
            ANY,
        ]
        out_specs = [tile_spec, whole(8, 128)]
        out_shape = [tile_shape, jax.ShapeDtypeStruct((8, 128), F32)]
    else:
        in_specs.append(pl.BlockSpec((SRC, FIRST, PTS), lambda s: (s, 0, 0)))
        out_specs = [tile_spec, pl.BlockSpec((FIRST_ROWS, LANES), lambda s: (0, s))]
        out_shape = [tile_shape, jax.ShapeDtypeStruct((FIRST_ROWS, steps * LANES), F32)]
    return pl.pallas_call(
        functools.partial(spread_kernel, e),
        grid=(steps,),
        in_specs=in_specs,
        out_specs=out_specs,
        out_shape=out_shape,
        scratch_shapes=[
            pltpu.VMEM((2, 9, 16, LANES), F32),
            pltpu.VMEM((1296, 256), F32),
            pltpu.VMEM((5 * TILE, 128), F32),
            pltpu.VMEM((2 * TILE, 640), BF),
        ],
        input_output_aliases={4: 0} if e else {},
        name="spread",
        **settings(20, 60),
    )(flags, damp, *args)


def finish_kernel(in_ref, behind, step_ref, res_ref, dir_ref, both, image):
    step = pl.program_id(0)
    rows = in_ref.shape[0] // NCL
    lane = iota((8, 128), 1)
    flat = in_ref.reshape(NDEV // 2 * 16, 128)
    for k in range(rows):
        r = step * rows + k
        share = jnp.sum(in_ref[NCL * k : NCL * k + NCL], axis=0)
        image[pl.ds(r, 16, stride=8), :] = share
        for t in range(3):
            at = NCL * 16 * k + 9 + t
            even = flat[pl.ds(at, 8, stride=32), :]
            odd = flat[pl.ds(at + 16, 8, stride=32), :]
            both[3 * r + t] = jnp.where(lane < CAM, even, pltpu.roll(odd, CAM, 1))

    @pl.when(step == pl.num_programs(0) - 1)
    def _():
        def total(values):
            return jnp.sum(sum(values), keepdims=True)

        rhs = [both[i] for i in range(8)] + [both[16]]
        diag = [both[8 + i] for i in range(8)] + [both[17]]
        product = [image[8 * i : 8 * i + 8] for i in range(9)]
        start = [a / b for a, b in zip(rhs, diag)]
        rz = total([a * b for a, b in zip(rhs, start)])
        alpha = rz / total([a * b for a, b in zip(start, product)])
        residual = [a - alpha * b for a, b in zip(rhs, product)]
        second = [a / b for a, b in zip(residual, diag)]
        beta = total([a * b for a, b in zip(residual, second)]) / rz
        values = (
            [alpha * a for a in start],
            residual,
            [a + beta * b for a, b in zip(second, start)],
        )
        for r in range(9):
            at = 128 * r + lane
            camera = at // 9
            which = at - 9 * camera
            for value, ref in zip(values, (step_ref, res_ref, dir_ref)):
                row = jnp.take_along_axis(value[0], camera, axis=1)
                for i in range(1, 9):
                    row = jnp.where(which == i, jnp.take_along_axis(value[i], camera, axis=1), row)
                ref[pl.ds(r, 8, stride=9), :] = row


def finish(incoming, behind):
    return pl.pallas_call(
        finish_kernel,
        grid=(2,),
        in_specs=[pl.BlockSpec((NDEV // 2, 16, 128), lambda s: (s, 0, 0)), ANY],
        out_specs=[whole(72, 128)] * 3,
        out_shape=[jax.ShapeDtypeStruct((72, 128), F32)] * 3,
        scratch_shapes=[pltpu.VMEM((24, 8, 128), F32), pltpu.VMEM((128, 128), F32)],
        name="finish",
        **settings(3, 63),
    )(incoming, behind)


def shards(jac_cam, jac_pt, resid, point_damp, cam_damp, obs_cluster, obs_slot):
    my_row = lax.axis_index("row")
    my_col = lax.axis_index("col")
    flags = (2 * my_row + jnp.arange(2) == my_col).astype(jnp.int32)
    flags = jnp.concatenate([flags, my_row[None].astype(jnp.int32)])
    damp = cam_damp.reshape(CAM, 9).T
    zeros = jnp.zeros((8, CAM), F32)
    damp = jnp.concatenate([zeros, damp[0:8], zeros[0:1], damp[8:9], zeros[0:6]], axis=0)
    first, dense, found = pack_first(
        jac_cam.transpose(1, 0, 2), jac_pt.transpose(1, 0, 2), resid, point_damp, obs_cluster.T,
        obs_slot,
    )
    first = exchange(first.reshape(NDEV, FIRST, PTS))
    second = exchange(pack_second(dense, found).reshape(NDEV, SECOND // 4, 4, PTS))
    tiles, one = spread(0, flags, cam_damp, (first,))
    two, share = cg_part(flags, one, second, damp)
    shares = exchange(share)
    tiles, token = spread(1, flags, cam_damp, (one, two, tiles, share))
    step, residual, direction = finish(shares, token)
    return (tiles[:, None], step.reshape(-1), residual.reshape(-1), direction.reshape(-1))


def solution(mesh):
    placed = (
        P(None, None, AXES),
        P(None, None, AXES),
        P(None, None, AXES),
        P(None, AXES),
        P("col", None),
        P(AXES, None),
        P(None, AXES),
    )
    return jax.shard_map(
        shards,
        mesh=mesh,
        in_specs=placed,
        out_specs=(P("row", "col", None, None), P(), P(), P()),
        check_vma=False,
    )
```

```python
import functools

import jax
import jax.numpy as jnp
from jax import lax
from jax.experimental import pallas as pl
from jax.experimental.pallas import tpu as pltpu
from jax.sharding import PartitionSpec as P

KOBS = 8
NCL = 16
CAP = 96
CAM = 64
TILE = 576
NROW = 8
NDEV = 128
PTS = 128
AXES = ("row", "col")
BF = jnp.bfloat16
F8 = jnp.float8_e4m3fn
F32 = jnp.float32
NT = (((1,), (1,)), ((), ()))
MIB = 1 << 20
SRC = 64
PAIRS = 8
LANES = SRC * CAP
GROUP = 3
ANY = pl.BlockSpec(memory_space=pl.ANY)


def iota(shape, dim):
    return lax.broadcasted_iota(jnp.int32, shape, dim)


def whole(*shape):
    return pl.BlockSpec(shape, lambda *_: (0,) * len(shape))


def settings(micros, mib):
    return dict(
        compiler_params=pltpu.CompilerParams(vmem_limit_bytes=mib * MIB),
        cost_estimate=pl.CostEstimate(
            flops=micros * 10**9, bytes_accessed=10**6, transcendentals=0
        ),
    )


def lanes_of(row, n):
    return jnp.broadcast_to(row, (n, row.shape[1]))


def whitened(jp, rs, damp):
    def inner(a, b):
        return jnp.sum(jp[0][a] * jp[0][b] + jp[1][a] * jp[1][b], axis=0, keepdims=True)

    laa = jnp.sqrt(inner(0, 0) + damp[0:1])
    lba = inner(1, 0) / laa
    lca = inner(2, 0) / laa
    lbb = jnp.sqrt(inner(1, 1) + damp[1:2] - lba * lba)
    lcb = (inner(2, 1) - lca * lba) / lbb
    lcc = jnp.sqrt(inner(2, 2) + damp[2:3] - lca * lca - lcb * lcb)

    def solve(a, b, c):
        x = a / laa
        y = (b - lba * x) / lbb
        return [x, y, (c - lca * x - lcb * y) / lcc]

    u = [solve(*jp[m]) for m in range(2)]
    grad = [
        jnp.sum(jp[0][a] * rs[0] + jp[1][a] * rs[1], axis=0, keepdims=True) for a in range(3)
    ]
    w = solve(*grad)
    q = [u[m][0] * w[0] + u[m][1] * w[1] + u[m][2] * w[2] - rs[m] for m in range(2)]
    return u, q


def hot(code, n):
    codes = lanes_of(code.astype(F32), n).astype(BF)
    ids = iota((n, code.shape[1]), 0).astype(F32).astype(BF)
    return jnp.where(codes == ids, jnp.ones((), BF), jnp.zeros((), BF))


def halves(value):
    high = value.astype(BF)
    return jnp.concatenate([high, (value - high.astype(F32)).astype(BF)], axis=0)


def chosen(named):
    upto = (iota((PTS, PTS), 0) <= iota((PTS, PTS), 1)).astype(F32).astype(BF)
    counts = jnp.dot(named.astype(BF), upto, preferred_element_type=F32)
    lane = iota(named.shape, 1)
    at = jnp.zeros(named.shape, jnp.int32)
    for jump in (64, 32, 16, 8, 4, 2, 1):
        seen = jnp.take_along_axis(counts, at + (jump - 1), axis=1)
        at = jnp.where(seen <= lane.astype(F32), at + jump, at)
    return jnp.where(lane.astype(F32) < counts[:, PTS - 1 : PTS], at, PTS)


def points_part(jc, jp, rs, damp, cl_ref, slot_ref, dense, found_ref, fields):
    cl, slot = cl_ref[...], slot_ref[...]
    u, q = whitened(
        [[jp[m * 3 + a] for a in range(3)] for m in range(2)],
        [rs[:, m, :] for m in range(2)],
        damp[...],
    )
    j0, j1 = jc[0], jc[9]
    top = jnp.maximum(jnp.abs(j0), jnp.abs(j1))
    some = top > 0.0
    safe = jnp.where(some, top, 1.0)
    x, y = j0 / safe, j1 / safe
    length = jnp.where(some, jnp.sqrt(x * x + y * y), 1.0)
    cs = jnp.where(some, x / length, 1.0)
    sn = jnp.where(some, y / length, 0.0)
    for i in range(9):
        a, b = jc[i], jc[9 + i]
        fields[i] = cs * a + sn * b
        if i:
            fields[8 + i] = cs * b - sn * a
    turned = [[], []]
    for a in range(3):
        turned[0].append(cs * u[0][a] + sn * u[1][a])
        turned[1].append(cs * u[1][a] - sn * u[0][a])
        fields[17 + a] = turned[0][a]
        fields[20 + a] = turned[1][a]
    fields[23] = slot.astype(F32)
    fields[24] = cs * q[0] + sn * q[1]
    fields[25] = cs * q[1] - sn * q[0]
    fields[26] = 1.0 - sum(v * v for v in turned[0])
    fields[27] = -2.0 * sum(v * w for v, w in zip(*turned))
    fields[28] = 1.0 - sum(v * v for v in turned[1])
    for e in range(2):
        ids = 2 * iota((NROW, PTS), 0) + e
        hits = [lanes_of(cl[k : k + 1], NROW) == ids for k in range(KOBS)]
        for f in range(29):
            value = jnp.full((NROW, PTS), -1.0 if f == 23 else 0.0, F32)
            for k in range(KOBS):
                value = jnp.where(hits[k], lanes_of(fields[f, k : k + 1, :], NROW), value)
            dense[f, e] = value
        found_ref[e] = chosen((dense[23, e] >= 0.0).astype(F32))


def mixed(side, mine, on):
    out = []
    for m in range(2):
        for n in range(2):
            v = sum(side[17 + 3 * m + a] * mine[17 + 3 * n + a] for a in range(3))
            out.append(on - v if m == n else -v)
    return out


def picked(dense, found_ref, pair, ec):
    found = lanes_of(found_ref[ec, pl.ds(pair, 1), :], NROW)
    pick = jnp.minimum(found, PTS - 1)
    same = [jnp.where(iota((NROW, PTS), 0) == pair, float(e == ec), 0.0) for e in range(2)]
    return found, same, lambda f, e: jnp.take_along_axis(dense[f, e], pick, axis=1)


def in_lists(rows, extra, slots):
    lane = iota((NROW, PTS), 1)
    rest = [jnp.zeros((NROW, PTS), F32)] * len(rows)
    for value, places in zip(extra, slots):
        for v, r in enumerate(places):
            rest[r] = pltpu.roll(value, 96 - 32 * v, 1)
    return [jnp.where(lane < CAP, a, b) for a, b in zip(rows, rest)]


FIRST_SLOTS = [(x, 8 + x, 16 + x) for x in range(8)] + [(24, 25, 26)]
SECOND_SLOTS = [(x, 6 + x, 12 + x) for x in range(6)]


def pack_first_kernel(jc, jp, rs, damp, cl, slot, out_ref, dense, found_ref, fields, kept):
    step = pl.program_id(0)

    @pl.when(step == 0)
    def _():
        points_part(jc, jp, rs, damp, cl, slot, dense, found_ref, fields)

    for part in range(PAIRS):
        pair = step * PAIRS + part
        for ec in range(2):
            found, same, take = picked(dense, found_ref, pair, ec)
            side = [take(f, 0) for f in range(24)]
            for f in range(24):
                kept[2 * part + ec, f] = take(f, 1) if ec else side[f]
            mine = [lanes_of(kept[2 * part + ec, f, pl.ds(pair, 1), :], NROW) for f in range(24)]
            list_slot = jnp.where(found < PTS, mine[23], -1.0)
            extra = [side[16], mine[16]] + mixed(side, mine, same[0]) + [side[23], list_slot]
            extra.append(take(23, 1))
            values = in_lists(side[0:16] + mine[0:16], extra, FIRST_SLOTS)
            for r in range(0, FIRST, 8):
                block = jnp.swapaxes(jnp.stack(values[r : r + 8], axis=0), 0, 1)
                out_ref[:, 2 * part + ec, r : r + 8, :] = block


def pack_second_kernel(dense, found_ref, out_ref, kept):
    step = pl.program_id(0)
    for part in range(PAIRS):
        pair = step * PAIRS + part
        for ec in range(2):
            _, same, take = picked(dense, found_ref, pair, ec)
            side = [take(f, 1) for f in range(23)]
            for f in range(17, 29):
                if f != 23:
                    kept[2 * part + ec, f] = take(f, ec)
            mine = {
                f: lanes_of(kept[2 * part + ec, f, pl.ds(pair, 1), :], NROW)
                for f in range(17, 29)
                if f != 23
            }
            rows = side[0:17] + [mine[24], mine[25], mine[26]]
            extra = [mine[27], mine[28]] + mixed(side, mine, same[1])
            values = in_lists(rows, extra, SECOND_SLOTS)
            values += values[0:4]
            for r in range(0, SECOND, 8):
                block = jnp.swapaxes(jnp.stack(values[r : r + 8], axis=0), 0, 1)
                out_ref[:, 2 * part + ec, r // 4] = block[:, 0:4]
                if r + 4 < SECOND:
                    out_ref[:, 2 * part + ec, r // 4 + 1] = block[:, 4:8]


def pack_first(*args):
    return pl.pallas_call(
        pack_first_kernel,
        grid=(NROW // PAIRS,),
        in_specs=[whole(*a.shape) for a in args],
        out_specs=[
            pl.BlockSpec((NROW, 2 * PAIRS, FIRST, PTS), lambda g: (0, g, 0, 0)),
            whole(29, 2, NROW, PTS),
            whole(2, NROW, PTS),
        ],
        out_shape=[
            jax.ShapeDtypeStruct((NROW, NCL, FIRST, PTS), F32),
            jax.ShapeDtypeStruct((29, 2, NROW, PTS), F32),
            jax.ShapeDtypeStruct((2, NROW, PTS), jnp.int32),
        ],
        scratch_shapes=[
            pltpu.VMEM((29, KOBS, PTS), F32),
            pltpu.VMEM((2 * PAIRS, 24, NROW, PTS), F32),
        ],
        name="pack_first",
        **settings(5, 60),
    )(*args)


def pack_second(dense, found):
    return pl.pallas_call(
        pack_second_kernel,
        grid=(NROW // PAIRS,),
        in_specs=[whole(29, 2, NROW, PTS), whole(2, NROW, PTS)],
        out_specs=pl.BlockSpec(
            (NROW, 2 * PAIRS, SECOND // 4, 4, PTS), lambda g: (0, g, 0, 0, 0)
        ),
        out_shape=jax.ShapeDtypeStruct((NROW, NCL, SECOND // 4, 4, PTS), F32),
        scratch_shapes=[pltpu.VMEM((2 * PAIRS, 29, NROW, PTS), F32)],
        name="pack_second",
        **settings(5, 60),
    )(dense, found)


def exchange(value):
    return lax.all_to_all(value, AXES, split_axis=0, concat_axis=0, tiled=True)


FIRST, FIRST_ROWS = 32, 41
SECOND, SECOND_ROWS = 20, 26


def joined(a, b, c):
    lane = iota(a.shape, 1)
    a, b, c = pltpu.roll(a, 32, 1), pltpu.roll(b, 64, 1), pltpu.roll(c, 96, 1)
    return jnp.where(lane < 32, a, jnp.where(lane < 64, b, c))


def lay(in_ref, rows_ref):
    full = iota(rows_ref.shape[0:1] + (PTS,), 1)
    for quarter in range(SRC // 4):
        pieces = []
        for s in range(quarter * 4, quarter * 4 + 4):
            if len(in_ref.shape) == 3:
                block = in_ref[s]
                rest = [joined(block[0:8], block[8:16], block[16:24])]
                rest.append(joined(block[24:25], block[25:26], block[26:27]))
            else:
                block = jnp.concatenate([in_ref[s, k] for k in range(SECOND // 4)], axis=0)
                rest = [joined(block[0:6], block[6:12], block[12:18])]
            pieces.append(jnp.concatenate([block] + rest, axis=0))
        r1, r2 = pltpu.roll(pieces[1], 96, 1), pltpu.roll(pieces[2], 64, 1)
        r3 = pltpu.roll(pieces[3], 32, 1)
        base = quarter * 384
        rows_ref[:, base : base + 128] = jnp.where(full < 96, pieces[0], r1)
        rows_ref[:, base + 128 : base + 256] = jnp.where(full < 64, r1, r2)
        rows_ref[:, base + 256 : base + 384] = jnp.where(full < 32, r2, r3)


def jacobian(rows_ref, at, last):
    first = iota((8, LANES), 0) == 0
    a1 = jnp.where(first, 0.0, rows_ref[at + 8 : at + 16])
    return rows_ref[at : at + 8], a1, rows_ref[at + 8 : at + 9], rows_ref[last : last + 1]


def side_of(e, one, two):
    if e:
        return jacobian(two, 0, 16), [two[22 + n : 23 + n] for n in range(4)], one[40:41]
    return jacobian(one, 0, 32), [one[34 + n : 35 + n] for n in range(4)], one[38:39]


def cg_kernel(flag_ref, one, in_ref, damp_ref, two, out_ref, keep1, keep2, hits, sums, image, kept):
    step = pl.program_id(0)
    steps = pl.num_programs(0)

    @pl.when(step == 0)
    def _():
        sums[...] = jnp.zeros_like(sums)

    lay(in_ref, two)
    a0, a1, l0, l1 = jacobian(one, 16, 33)
    q0, q1 = two[17:18], two[18:19]
    m0, m1, m2 = two[19:20], two[20:21], two[21:22]
    terms = [
        a0 * lanes_of(q0, 8) + a1 * lanes_of(q1, 8),
        a0 * a0 * lanes_of(m0, 8) + a0 * a1 * lanes_of(m1, 8) + a1 * a1 * lanes_of(m2, 8),
        l0 * q0 + l1 * q1,
        l0 * l0 * m0 + l0 * l1 * m1 + l1 * l1 * m2,
        jnp.zeros((14, LANES), F32),
    ]
    hit = hot(one[39:40].astype(jnp.int32), CAM)
    hits[step] = hit
    keep1[step] = one[...]
    keep2[step] = two[...]
    sums[...] += lax.dot_general(
        halves(jnp.concatenate(terms, axis=0)), hit, NT, preferred_element_type=F32
    )

    @pl.when(step == steps - 1)
    def _():
        damp = damp_ref[...]
        total = sums[0:24] + sums[32:56] + damp
        kept[...] = jnp.concatenate([total, jnp.zeros_like(total)], axis=1)
        x8, x9 = total[0:8] / total[8:16], total[16:17] / total[17:18]
        x = halves(jnp.concatenate([x8, x9, jnp.zeros((7, CAM), F32)], axis=0))
        parts, spots = [[], []], [[], []]
        for at in range(NDEV // SRC):
            rows1, rows2 = keep1.at[at], keep2.at[at]
            got = jnp.dot(x, hits[at], preferred_element_type=F32)
            got = got[0:16] + got[16:32]
            a0, a1, l0, l1 = jacobian(rows1, 16, 33)
            v0 = jnp.sum(a0 * got[0:8], axis=0, keepdims=True) + l0 * got[8:9]
            v1 = jnp.sum(a1 * got[0:8], axis=0, keepdims=True) + l1 * got[8:9]
            for e in range(2):
                (a0, a1, l0, l1), m, slot = side_of(e, rows1, rows2)
                z0, z1 = m[0] * v0 + m[1] * v1, m[2] * v0 + m[3] * v1
                out8 = a0 * lanes_of(z0, 8) + a1 * lanes_of(z1, 8)
                terms = [out8, l0 * z0 + l1 * z1, jnp.zeros((7, LANES), F32)]
                parts[e].append(halves(jnp.concatenate(terms, axis=0)))
                spots[e].append(hot(slot.astype(jnp.int32), CAM))

        for e in range(2):
            image[e] = lax.dot_general(
                jnp.concatenate(parts[e], axis=1),
                jnp.concatenate(spots[e], axis=1),
                NT,
                preferred_element_type=F32,
            )
        extra = jnp.concatenate([damp[8:16] * x8, damp[17:18] * x9, jnp.zeros((7, CAM), F32)], axis=0)
        y = [
            image[e, 0:16] + image[e, 16:32] + jnp.where(flag_ref[e] == 1, extra, 0.0)
            for e in range(2)
        ]
        y = jnp.concatenate(y, axis=1)
        part = kept[pl.ds(3 * flag_ref[2], 3), :]
        block = jnp.concatenate([y[0:9], part, jnp.zeros((4, 128), F32)], axis=0)
        out_ref[...] = jnp.broadcast_to(block[None], (NDEV, 16, 128))

def cg_part(flags, one, incoming, damp):
    steps = NDEV // SRC
    return pl.pallas_call(
        cg_kernel,
        grid=(steps,),
        in_specs=[
            pl.BlockSpec(memory_space=pltpu.SMEM),
            pl.BlockSpec((FIRST_ROWS, LANES), lambda s: (0, s)),
            pl.BlockSpec((SRC, SECOND // 4, 4, PTS), lambda s: (s, 0, 0, 0)),
            whole(24, CAM),
        ],
        out_specs=[
            pl.BlockSpec((SECOND_ROWS, LANES), lambda s: (0, s)),
            whole(NDEV, 16, 128),
        ],
        out_shape=[
            jax.ShapeDtypeStruct((SECOND_ROWS, steps * LANES), F32),
            jax.ShapeDtypeStruct((NDEV, 16, 128), F32),
        ],
        scratch_shapes=[
            pltpu.VMEM((steps, FIRST_ROWS, LANES), F32),
            pltpu.VMEM((steps, SECOND_ROWS, LANES), F32),
            pltpu.VMEM((steps, CAM, LANES), BF),
            pltpu.VMEM((64, CAM), F32),
            pltpu.VMEM((2, 32, CAM), F32),
            pltpu.VMEM((24, 128), F32),
        ],
        name="cg",
        **settings(6, 63),
    )(flags, one, incoming, damp)


SCALE = 2048.0


def add_products(e, one, two, prod, acc):
    def split(value):
        high = value.astype(BF).astype(F32)
        return high, value - high

    (a0, a1, last0, last1), middle, slot_a = side_of(e, one, two)
    cam0, cam1, cam_last0, cam_last1 = jacobian(one, 16, 33)
    t, t_last = [], []
    for m in range(2):
        m0, m1 = middle[2 * m] * SCALE, middle[2 * m + 1] * SCALE
        t.append(lanes_of(m0, 8) * cam0 + lanes_of(m1, 8) * cam1)
        t_last.append(m0 * cam_last0 + m1 * cam_last1)
    for j in range(9):
        t0 = t[0][j : j + 1] if j < 8 else t_last[0]
        t1 = t[1][j : j + 1] if j < 8 else t_last[1]
        high, low = split(a0 * lanes_of(t0, 8) + a1 * lanes_of(t1, 8))
        prod[0, j, 0:8] = high
        prod[1, j, 0:8] = low
        high, low = split(last0 * t0 + last1 * t1)
        prod[0, j, 8:9] = high
        prod[1, j, 8:9] = low
    slot_a, slot_c = slot_a.astype(jnp.int32), one[39:40].astype(jnp.int32)
    both = jnp.minimum(slot_a, slot_c) >= 0
    code = jnp.where(both, (slot_a >> 4) * CAM + slot_c, -1)
    onehot = hot(code, 256)
    mask = hot(slot_a & 15, 16)
    n = GROUP * 144
    onehot8 = onehot.astype(F8)
    for g in range(9 // GROUP):
        parts = [[], []]
        for h in range(2):
            for j in range(g * GROUP, (g + 1) * GROUP):
                for i in range(9):
                    parts[h].append(lanes_of(prod[h, j, i : i + 1], 16).astype(BF) * mask)
        high = jnp.concatenate(parts[0], axis=0)
        low = jnp.concatenate(parts[1], axis=0).astype(F8)
        got = lax.dot_general(high, onehot, NT, preferred_element_type=F32)
        rest = lax.dot_general(low, onehot8, NT, preferred_element_type=F32)
        acc[g * n : (g + 1) * n, :] += got + rest


def assemble(read, flag, damp_ref, out_ref, stage, wide_ref):
    source = iota((640, 640), 0)
    place = iota((640, 640), 1) == 9 * (source % CAM) + source // CAM
    place = (place & (source < TILE)).astype(F32).astype(BF)
    lane = iota((144, PTS), 1)
    for u in range(4):
        base = (u // 2) * 128
        tiles = []
        for jj in range(5):
            even = read(2 * jj, base)
            if u % 2:
                even = pltpu.roll(even, 64, 1)
            if jj < 4:
                odd = read(2 * jj + 1, base)
                if u % 2 == 0:
                    odd = pltpu.roll(odd, 64, 1)
                even = jnp.where(lane < CAM, even, odd)
            tiles.append(even)
        full = jnp.concatenate(tiles, axis=1) * (1.0 / SCALE)
        high = full.astype(BF)
        wide_ref[144 * u : 144 * u + 144] = high
        wide_ref[TILE + 144 * u : TILE + 144 * u + 144] = (full - high.astype(F32)).astype(BF)
    got = jnp.dot(wide_ref[...], place, preferred_element_type=F32)
    got = got[:TILE] + got[TILE:]
    for u in range(4):
        for tile in range(5):
            for i in range(9):
                at = 144 * u + 16 * i
                piece = got[at : at + 16, 128 * tile : 128 * tile + 128]
                stage[pl.ds(TILE * tile + 144 * u + i, 16, stride=9), :] = piece
    for tile in range(5):
        wide = min(128, TILE - 128 * tile)
        block = stage[TILE * tile : TILE * tile + TILE, 0:wide]
        out_ref[0, :, 128 * tile : 128 * tile + wide] = block

    @pl.when(flag == 1)
    def _():
        same = iota((TILE, TILE), 0) == iota((TILE, TILE), 1)
        out_ref[0] += jnp.where(same, jnp.broadcast_to(damp_ref[...], (TILE, TILE)), 0.0)


def spread_kernel(e, flag_ref, damp_ref, *refs):
    if e:
        one, two, out_ref, token, prod, acc, stage, wide_ref = refs[0], refs[1], *refs[4:]
    else:
        in_ref, out_ref, one, prod, acc, stage, wide_ref = refs
    step = pl.program_id(0)

    @pl.when(step == 0)
    def _():
        acc[...] = jnp.zeros_like(acc)

    if e:
        add_products(1, one, two, prod, acc)
    else:
        lay(in_ref, one)
        add_products(0, one, None, prod, acc)

    @pl.when(step == pl.num_programs(0) - 1)
    def _():
        def read(j, base):
            return acc[144 * j : 144 * j + 144, base : base + 128]

        assemble(read, flag_ref[e], damp_ref, out_ref, stage, wide_ref)
        if e:
            token[...] = jnp.zeros_like(token)


def spread(e, flags, damp, args):
    steps = NDEV // SRC
    in_specs = [pl.BlockSpec(memory_space=pltpu.SMEM), whole(1, TILE)]
    tile_spec = pl.BlockSpec((1, TILE, TILE), lambda s: (e, 0, 0))
    tile_shape = jax.ShapeDtypeStruct((2, TILE, TILE), F32)
    if e:
        in_specs += [
            pl.BlockSpec((FIRST_ROWS, LANES), lambda s: (0, s)),
            pl.BlockSpec((SECOND_ROWS, LANES), lambda s: (0, s)),
            ANY,
            ANY,
        ]
        out_specs = [tile_spec, whole(8, 128)]
        out_shape = [tile_shape, jax.ShapeDtypeStruct((8, 128), F32)]
    else:
        in_specs.append(pl.BlockSpec((SRC, FIRST, PTS), lambda s: (s, 0, 0)))
        out_specs = [tile_spec, pl.BlockSpec((FIRST_ROWS, LANES), lambda s: (0, s))]
        out_shape = [tile_shape, jax.ShapeDtypeStruct((FIRST_ROWS, steps * LANES), F32)]
    return pl.pallas_call(
        functools.partial(spread_kernel, e),
        grid=(steps,),
        in_specs=in_specs,
        out_specs=out_specs,
        out_shape=out_shape,
        scratch_shapes=[
            pltpu.VMEM((2, 9, 16, LANES), F32),
            pltpu.VMEM((1296, 256), F32),
            pltpu.VMEM((5 * TILE, 128), F32),
            pltpu.VMEM((2 * TILE, 640), BF),
        ],
        input_output_aliases={4: 0} if e else {},
        name="spread",
        **settings(20, 60),
    )(flags, damp, *args)


def finish_kernel(in_ref, behind, step_ref, res_ref, dir_ref, both, image):
    step = pl.program_id(0)
    rows = in_ref.shape[0] // NCL
    lane = iota((8, 128), 1)
    flat = in_ref.reshape(NDEV // 2 * 16, 128)
    for k in range(rows):
        r = step * rows + k
        share = jnp.sum(in_ref[NCL * k : NCL * k + NCL], axis=0)
        image[pl.ds(r, 16, stride=8), :] = share
        for t in range(3):
            at = NCL * 16 * k + 9 + t
            even = flat[pl.ds(at, 8, stride=32), :]
            odd = flat[pl.ds(at + 16, 8, stride=32), :]
            both[3 * r + t] = jnp.where(lane < CAM, even, pltpu.roll(odd, CAM, 1))

    @pl.when(step == pl.num_programs(0) - 1)
    def _():
        def total(values):
            return jnp.sum(sum(values), keepdims=True)

        rhs = [both[i] for i in range(8)] + [both[16]]
        diag = [both[8 + i] for i in range(8)] + [both[17]]
        product = [image[8 * i : 8 * i + 8] for i in range(9)]
        start = [a / b for a, b in zip(rhs, diag)]
        rz = total([a * b for a, b in zip(rhs, start)])
        alpha = rz / total([a * b for a, b in zip(start, product)])
        residual = [a - alpha * b for a, b in zip(rhs, product)]
        second = [a / b for a, b in zip(residual, diag)]
        beta = total([a * b for a, b in zip(residual, second)]) / rz
        values = (
            [alpha * a for a in start],
            residual,
            [a + beta * b for a, b in zip(second, start)],
        )
        for r in range(9):
            at = 128 * r + lane
            camera = at // 9
            which = at - 9 * camera
            for value, ref in zip(values, (step_ref, res_ref, dir_ref)):
                row = jnp.take_along_axis(value[0], camera, axis=1)
                for i in range(1, 9):
                    row = jnp.where(which == i, jnp.take_along_axis(value[i], camera, axis=1), row)
                ref[pl.ds(r, 8, stride=9), :] = row


def finish(incoming, behind):
    return pl.pallas_call(
        finish_kernel,
        grid=(2,),
        in_specs=[pl.BlockSpec((NDEV // 2, 16, 128), lambda s: (s, 0, 0)), ANY],
        out_specs=[whole(72, 128)] * 3,
        out_shape=[jax.ShapeDtypeStruct((72, 128), F32)] * 3,
        scratch_shapes=[pltpu.VMEM((24, 8, 128), F32), pltpu.VMEM((128, 128), F32)],
        name="finish",
        **settings(3, 63),
    )(incoming, behind)


def shards(jac_cam, jac_pt, resid, point_damp, cam_damp, obs_cluster, obs_slot):
    my_row = lax.axis_index("row")
    my_col = lax.axis_index("col")
    flags = (2 * my_row + jnp.arange(2) == my_col).astype(jnp.int32)
    flags = jnp.concatenate([flags, my_row[None].astype(jnp.int32)])
    damp = cam_damp.reshape(CAM, 9).T
    zeros = jnp.zeros((8, CAM), F32)
    damp = jnp.concatenate([zeros, damp[0:8], zeros[0:1], damp[8:9], zeros[0:6]], axis=0)
    first, dense, found = pack_first(
        jac_cam.transpose(1, 0, 2), jac_pt.transpose(1, 0, 2), resid, point_damp, obs_cluster.T,
        obs_slot,
    )
    first = exchange(first.reshape(NDEV, FIRST, PTS))
    second = exchange(pack_second(dense, found).reshape(NDEV, SECOND // 4, 4, PTS))
    tiles, one = spread(0, flags, cam_damp, (first,))
    two, share = cg_part(flags, one, second, damp)
    shares = exchange(share)
    tiles, token = spread(1, flags, cam_damp, (one, two, tiles, share))
    step, residual, direction = finish(shares, token)
    return (tiles[:, None], step.reshape(-1), residual.reshape(-1), direction.reshape(-1))


def solution(mesh):
    placed = (
        P(None, None, AXES),
        P(None, None, AXES),
        P(None, None, AXES),
        P(None, AXES),
        P("col", None),
        P(AXES, None),
        P(None, AXES),
    )
    return jax.shard_map(
        shards,
        mesh=mesh,
        in_specs=placed,
        out_specs=(P("row", "col", None, None), P(), P(), P()),
        check_vma=False,
    )
```

```python
import functools

import jax
import jax.numpy as jnp
from jax import lax
from jax.experimental import pallas as pl
from jax.experimental.pallas import tpu as pltpu
from jax.sharding import PartitionSpec as P

KOBS = 8
NCL = 16
CAP = 96
CAM = 64
TILE = 576
NROW = 8
NDEV = 128
PTS = 128
AXES = ("row", "col")
BF = jnp.bfloat16
F8 = jnp.float8_e4m3fn
F32 = jnp.float32
NT = (((1,), (1,)), ((), ()))
MIB = 1 << 20
SRC = 64
PAIRS = 8
LANES = SRC * CAP
GROUP = 3
ANY = pl.BlockSpec(memory_space=pl.ANY)


def iota(shape, dim):
    return lax.broadcasted_iota(jnp.int32, shape, dim)


def whole(*shape):
    return pl.BlockSpec(shape, lambda *_: (0,) * len(shape))


def settings(micros, mib):
    return dict(
        compiler_params=pltpu.CompilerParams(vmem_limit_bytes=mib * MIB),
        cost_estimate=pl.CostEstimate(
            flops=micros * 10**9, bytes_accessed=10**6, transcendentals=0
        ),
    )


def lanes_of(row, n):
    return jnp.broadcast_to(row, (n, row.shape[1]))


def whitened(jp, rs, damp):
    def inner(a, b):
        return jnp.sum(jp[0][a] * jp[0][b] + jp[1][a] * jp[1][b], axis=0, keepdims=True)

    laa = jnp.sqrt(inner(0, 0) + damp[0:1])
    lba = inner(1, 0) / laa
    lca = inner(2, 0) / laa
    lbb = jnp.sqrt(inner(1, 1) + damp[1:2] - lba * lba)
    lcb = (inner(2, 1) - lca * lba) / lbb
    lcc = jnp.sqrt(inner(2, 2) + damp[2:3] - lca * lca - lcb * lcb)

    def solve(a, b, c):
        x = a / laa
        y = (b - lba * x) / lbb
        return [x, y, (c - lca * x - lcb * y) / lcc]

    u = [solve(*jp[m]) for m in range(2)]
    grad = [
        jnp.sum(jp[0][a] * rs[0] + jp[1][a] * rs[1], axis=0, keepdims=True) for a in range(3)
    ]
    w = solve(*grad)
    q = [u[m][0] * w[0] + u[m][1] * w[1] + u[m][2] * w[2] - rs[m] for m in range(2)]
    return u, q


def hot(code, n):
    codes = lanes_of(code.astype(F32), n).astype(BF)
    ids = iota((n, code.shape[1]), 0).astype(F32).astype(BF)
    return jnp.where(codes == ids, jnp.ones((), BF), jnp.zeros((), BF))


def halves(value):
    high = value.astype(BF)
    return jnp.concatenate([high, (value - high.astype(F32)).astype(BF)], axis=0)


def chosen(named):
    upto = (iota((PTS, PTS), 0) <= iota((PTS, PTS), 1)).astype(F32).astype(BF)
    counts = jnp.dot(named.astype(BF), upto, preferred_element_type=F32)
    lane = iota(named.shape, 1)
    at = jnp.zeros(named.shape, jnp.int32)
    for jump in (64, 32, 16, 8, 4, 2, 1):
        seen = jnp.take_along_axis(counts, at + (jump - 1), axis=1)
        at = jnp.where(seen <= lane.astype(F32), at + jump, at)
    return jnp.where(lane.astype(F32) < counts[:, PTS - 1 : PTS], at, PTS)


def points_part(jc, jp, rs, damp, cl_ref, slot_ref, dense, found_ref, fields):
    cl, slot = cl_ref[...], slot_ref[...]
    u, q = whitened(
        [[jp[m * 3 + a] for a in range(3)] for m in range(2)],
        [rs[:, m, :] for m in range(2)],
        damp[...],
    )
    j0, j1 = jc[0], jc[9]
    top = jnp.maximum(jnp.abs(j0), jnp.abs(j1))
    some = top > 0.0
    safe = jnp.where(some, top, 1.0)
    x, y = j0 / safe, j1 / safe
    length = jnp.where(some, jnp.sqrt(x * x + y * y), 1.0)
    cs = jnp.where(some, x / length, 1.0)
    sn = jnp.where(some, y / length, 0.0)
    for i in range(9):
        a, b = jc[i], jc[9 + i]
        fields[i] = cs * a + sn * b
        if i:
            fields[8 + i] = cs * b - sn * a
    turned = [[], []]
    for a in range(3):
        turned[0].append(cs * u[0][a] + sn * u[1][a])
        turned[1].append(cs * u[1][a] - sn * u[0][a])
        fields[17 + a] = turned[0][a]
        fields[20 + a] = turned[1][a]
    fields[23] = slot.astype(F32)
    fields[24] = cs * q[0] + sn * q[1]
    fields[25] = cs * q[1] - sn * q[0]
    fields[26] = 1.0 - sum(v * v for v in turned[0])
    fields[27] = -2.0 * sum(v * w for v, w in zip(*turned))
    fields[28] = 1.0 - sum(v * v for v in turned[1])
    for e in range(2):
        ids = 2 * iota((NROW, PTS), 0) + e
        hits = [lanes_of(cl[k : k + 1], NROW) == ids for k in range(KOBS)]
        for f in range(29):
            value = jnp.full((NROW, PTS), -1.0 if f == 23 else 0.0, F32)
            for k in range(KOBS):
                value = jnp.where(hits[k], lanes_of(fields[f, k : k + 1, :], NROW), value)
            dense[f, e] = value
        found_ref[e] = chosen((dense[23, e] >= 0.0).astype(F32))


def mixed(side, mine, on):
    out = []
    for m in range(2):
        for n in range(2):
            v = sum(side[17 + 3 * m + a] * mine[17 + 3 * n + a] for a in range(3))
            out.append(on - v if m == n else -v)
    return out


def picked(dense, found_ref, pair, ec):
    found = lanes_of(found_ref[ec, pl.ds(pair, 1), :], NROW)
    pick = jnp.minimum(found, PTS - 1)
    same = [jnp.where(iota((NROW, PTS), 0) == pair, float(e == ec), 0.0) for e in range(2)]
    return found, same, lambda f, e: jnp.take_along_axis(dense[f, e], pick, axis=1)


def in_lists(rows, extra, slots):
    lane = iota((NROW, PTS), 1)
    rest = [jnp.zeros((NROW, PTS), F32)] * len(rows)
    for value, places in zip(extra, slots):
        for v, r in enumerate(places):
            rest[r] = pltpu.roll(value, 96 - 32 * v, 1)
    return [jnp.where(lane < CAP, a, b) for a, b in zip(rows, rest)]


FIRST_SLOTS = [(x, 8 + x, 16 + x) for x in range(8)] + [(24, 25, 26)]
SECOND_SLOTS = [(x, 6 + x, 12 + x) for x in range(6)]


def pack_first_kernel(jc, jp, rs, damp, cl, slot, out_ref, dense, found_ref, fields, kept):
    step = pl.program_id(0)

    @pl.when(step == 0)
    def _():
        points_part(jc, jp, rs, damp, cl, slot, dense, found_ref, fields)

    for part in range(PAIRS):
        pair = step * PAIRS + part
        for ec in range(2):
            found, same, take = picked(dense, found_ref, pair, ec)
            side = [take(f, 0) for f in range(24)]
            for f in range(24):
                kept[2 * part + ec, f] = take(f, 1) if ec else side[f]
            mine = [lanes_of(kept[2 * part + ec, f, pl.ds(pair, 1), :], NROW) for f in range(24)]
            list_slot = jnp.where(found < PTS, mine[23], -1.0)
            extra = [side[16], mine[16]] + mixed(side, mine, same[0]) + [side[23], list_slot]
            extra.append(take(23, 1))
            values = in_lists(side[0:16] + mine[0:16], extra, FIRST_SLOTS)
            for r in range(0, FIRST, 8):
                block = jnp.swapaxes(jnp.stack(values[r : r + 8], axis=0), 0, 1)
                out_ref[:, 2 * part + ec, r : r + 8, :] = block


def pack_second_kernel(dense, found_ref, out_ref, kept):
    step = pl.program_id(0)
    for part in range(PAIRS):
        pair = step * PAIRS + part
        for ec in range(2):
            _, same, take = picked(dense, found_ref, pair, ec)
            side = [take(f, 1) for f in range(23)]
            for f in range(17, 29):
                if f != 23:
                    kept[2 * part + ec, f] = take(f, ec)
            mine = {
                f: lanes_of(kept[2 * part + ec, f, pl.ds(pair, 1), :], NROW)
                for f in range(17, 29)
                if f != 23
            }
            rows = side[0:17] + [mine[24], mine[25], mine[26]]
            extra = [mine[27], mine[28]] + mixed(side, mine, same[1])
            values = in_lists(rows, extra, SECOND_SLOTS)
            values += values[0:4]
            for r in range(0, SECOND, 8):
                block = jnp.swapaxes(jnp.stack(values[r : r + 8], axis=0), 0, 1)
                out_ref[:, 2 * part + ec, r // 4] = block[:, 0:4]
                if r + 4 < SECOND:
                    out_ref[:, 2 * part + ec, r // 4 + 1] = block[:, 4:8]


def pack_first(*args):
    return pl.pallas_call(
        pack_first_kernel,
        grid=(NROW // PAIRS,),
        in_specs=[whole(*a.shape) for a in args],
        out_specs=[
            pl.BlockSpec((NROW, 2 * PAIRS, FIRST, PTS), lambda g: (0, g, 0, 0)),
            whole(29, 2, NROW, PTS),
            whole(2, NROW, PTS),
        ],
        out_shape=[
            jax.ShapeDtypeStruct((NROW, NCL, FIRST, PTS), F32),
            jax.ShapeDtypeStruct((29, 2, NROW, PTS), F32),
            jax.ShapeDtypeStruct((2, NROW, PTS), jnp.int32),
        ],
        scratch_shapes=[
            pltpu.VMEM((29, KOBS, PTS), F32),
            pltpu.VMEM((2 * PAIRS, 24, NROW, PTS), F32),
        ],
        name="pack_first",
        **settings(5, 60),
    )(*args)


def pack_second(dense, found):
    return pl.pallas_call(
        pack_second_kernel,
        grid=(NROW // PAIRS,),
        in_specs=[whole(29, 2, NROW, PTS), whole(2, NROW, PTS)],
        out_specs=pl.BlockSpec(
            (NROW, 2 * PAIRS, SECOND // 4, 4, PTS), lambda g: (0, g, 0, 0, 0)
        ),
        out_shape=jax.ShapeDtypeStruct((NROW, NCL, SECOND // 4, 4, PTS), F32),
        scratch_shapes=[pltpu.VMEM((2 * PAIRS, 29, NROW, PTS), F32)],
        name="pack_second",
        **settings(5, 60),
    )(dense, found)


def exchange(value):
    return lax.all_to_all(value, AXES, split_axis=0, concat_axis=0, tiled=True)


FIRST, FIRST_ROWS = 32, 41
SECOND, SECOND_ROWS = 20, 26


def joined(a, b, c):
    lane = iota(a.shape, 1)
    a, b, c = pltpu.roll(a, 32, 1), pltpu.roll(b, 64, 1), pltpu.roll(c, 96, 1)
    return jnp.where(lane < 32, a, jnp.where(lane < 64, b, c))


def lay(in_ref, rows_ref):
    full = iota(rows_ref.shape[0:1] + (PTS,), 1)
    for quarter in range(SRC // 4):
        pieces = []
        for s in range(quarter * 4, quarter * 4 + 4):
            if len(in_ref.shape) == 3:
                block = in_ref[s]
                rest = [joined(block[0:8], block[8:16], block[16:24])]
                rest.append(joined(block[24:25], block[25:26], block[26:27]))
            else:
                block = jnp.concatenate([in_ref[s, k] for k in range(SECOND // 4)], axis=0)
                rest = [joined(block[0:6], block[6:12], block[12:18])]
            pieces.append(jnp.concatenate([block] + rest, axis=0))
        r1, r2 = pltpu.roll(pieces[1], 96, 1), pltpu.roll(pieces[2], 64, 1)
        r3 = pltpu.roll(pieces[3], 32, 1)
        base = quarter * 384
        rows_ref[:, base : base + 128] = jnp.where(full < 96, pieces[0], r1)
        rows_ref[:, base + 128 : base + 256] = jnp.where(full < 64, r1, r2)
        rows_ref[:, base + 256 : base + 384] = jnp.where(full < 32, r2, r3)


def jacobian(rows_ref, at, last):
    first = iota((8, LANES), 0) == 0
    a1 = jnp.where(first, 0.0, rows_ref[at + 8 : at + 16])
    return rows_ref[at : at + 8], a1, rows_ref[at + 8 : at + 9], rows_ref[last : last + 1]


def side_of(e, one, two):
    if e:
        return jacobian(two, 0, 16), [two[22 + n : 23 + n] for n in range(4)], one[40:41]
    return jacobian(one, 0, 32), [one[34 + n : 35 + n] for n in range(4)], one[38:39]


def cg_kernel(flag_ref, one, in_ref, damp_ref, two, out_ref, keep1, keep2, hits, sums, image, kept):
    step = pl.program_id(0)
    steps = pl.num_programs(0)

    @pl.when(step == 0)
    def _():
        sums[...] = jnp.zeros_like(sums)

    lay(in_ref, two)
    a0, a1, l0, l1 = jacobian(one, 16, 33)
    q0, q1 = two[17:18], two[18:19]
    m0, m1, m2 = two[19:20], two[20:21], two[21:22]
    terms = [
        a0 * lanes_of(q0, 8) + a1 * lanes_of(q1, 8),
        a0 * a0 * lanes_of(m0, 8) + a0 * a1 * lanes_of(m1, 8) + a1 * a1 * lanes_of(m2, 8),
        l0 * q0 + l1 * q1,
        l0 * l0 * m0 + l0 * l1 * m1 + l1 * l1 * m2,
        jnp.zeros((14, LANES), F32),
    ]
    hit = hot(one[39:40].astype(jnp.int32), CAM)
    hits[step] = hit
    keep1[step] = one[...]
    keep2[step] = two[...]
    sums[...] += lax.dot_general(
        halves(jnp.concatenate(terms, axis=0)), hit, NT, preferred_element_type=F32
    )

    @pl.when(step == steps - 1)
    def _():
        damp = damp_ref[...]
        total = sums[0:24] + sums[32:56] + damp
        kept[...] = jnp.concatenate([total, jnp.zeros_like(total)], axis=1)
        x8, x9 = total[0:8] / total[8:16], total[16:17] / total[17:18]
        x = halves(jnp.concatenate([x8, x9, jnp.zeros((7, CAM), F32)], axis=0))
        parts, spots = [[], []], [[], []]
        for at in range(NDEV // SRC):
            rows1, rows2 = keep1.at[at], keep2.at[at]
            got = jnp.dot(x, hits[at], preferred_element_type=F32)
            got = got[0:16] + got[16:32]
            a0, a1, l0, l1 = jacobian(rows1, 16, 33)
            v0 = jnp.sum(a0 * got[0:8], axis=0, keepdims=True) + l0 * got[8:9]
            v1 = jnp.sum(a1 * got[0:8], axis=0, keepdims=True) + l1 * got[8:9]
            for e in range(2):
                (a0, a1, l0, l1), m, slot = side_of(e, rows1, rows2)
                z0, z1 = m[0] * v0 + m[1] * v1, m[2] * v0 + m[3] * v1
                out8 = a0 * lanes_of(z0, 8) + a1 * lanes_of(z1, 8)
                terms = [out8, l0 * z0 + l1 * z1, jnp.zeros((7, LANES), F32)]
                parts[e].append(halves(jnp.concatenate(terms, axis=0)))
                spots[e].append(hot(slot.astype(jnp.int32), CAM))

        for e in range(2):
            image[e] = lax.dot_general(
                jnp.concatenate(parts[e], axis=1),
                jnp.concatenate(spots[e], axis=1),
                NT,
                preferred_element_type=F32,
            )
        extra = jnp.concatenate([damp[8:16] * x8, damp[17:18] * x9, jnp.zeros((7, CAM), F32)], axis=0)
        y = [
            image[e, 0:16] + image[e, 16:32] + jnp.where(flag_ref[e] == 1, extra, 0.0)
            for e in range(2)
        ]
        y = jnp.concatenate(y, axis=1)
        part = kept[pl.ds(3 * flag_ref[2], 3), :]
        block = jnp.concatenate([y[0:9], part, jnp.zeros((4, 128), F32)], axis=0)
        out_ref[...] = jnp.broadcast_to(block[None], (NDEV, 16, 128))

def cg_part(flags, one, incoming, damp):
    steps = NDEV // SRC
    return pl.pallas_call(
        cg_kernel,
        grid=(steps,),
        in_specs=[
            pl.BlockSpec(memory_space=pltpu.SMEM),
            pl.BlockSpec((FIRST_ROWS, LANES), lambda s: (0, s)),
            pl.BlockSpec((SRC, SECOND // 4, 4, PTS), lambda s: (s, 0, 0, 0)),
            whole(24, CAM),
        ],
        out_specs=[
            pl.BlockSpec((SECOND_ROWS, LANES), lambda s: (0, s)),
            whole(NDEV, 16, 128),
        ],
        out_shape=[
            jax.ShapeDtypeStruct((SECOND_ROWS, steps * LANES), F32),
            jax.ShapeDtypeStruct((NDEV, 16, 128), F32),
        ],
        scratch_shapes=[
            pltpu.VMEM((steps, FIRST_ROWS, LANES), F32),
            pltpu.VMEM((steps, SECOND_ROWS, LANES), F32),
            pltpu.VMEM((steps, CAM, LANES), BF),
            pltpu.VMEM((64, CAM), F32),
            pltpu.VMEM((2, 32, CAM), F32),
            pltpu.VMEM((24, 128), F32),
        ],
        name="cg",
        **settings(6, 63),
    )(flags, one, incoming, damp)


SCALE = 2048.0


def add_products(e, one, two, prod, acc):
    def split(value):
        high = value.astype(BF).astype(F32)
        return high, value - high

    (a0, a1, last0, last1), middle, slot_a = side_of(e, one, two)
    cam0, cam1, cam_last0, cam_last1 = jacobian(one, 16, 33)
    t, t_last = [], []
    for m in range(2):
        m0, m1 = middle[2 * m] * SCALE, middle[2 * m + 1] * SCALE
        t.append(lanes_of(m0, 8) * cam0 + lanes_of(m1, 8) * cam1)
        t_last.append(m0 * cam_last0 + m1 * cam_last1)
    for j in range(9):
        t0 = t[0][j : j + 1] if j < 8 else t_last[0]
        t1 = t[1][j : j + 1] if j < 8 else t_last[1]
        high, low = split(a0 * lanes_of(t0, 8) + a1 * lanes_of(t1, 8))
        prod[0, j, 0:8] = high
        prod[1, j, 0:8] = low
        high, low = split(last0 * t0 + last1 * t1)
        prod[0, j, 8:9] = high
        prod[1, j, 8:9] = low
    slot_a, slot_c = slot_a.astype(jnp.int32), one[39:40].astype(jnp.int32)
    both = jnp.minimum(slot_a, slot_c) >= 0
    code = jnp.where(both, (slot_a >> 4) * CAM + slot_c, -1)
    onehot = hot(code, 256)
    mask = hot(slot_a & 15, 16)
    n = GROUP * 144
    onehot8 = onehot.astype(F8)
    for g in range(9 // GROUP):
        parts = [[], []]
        for h in range(2):
            for j in range(g * GROUP, (g + 1) * GROUP):
                for i in range(9):
                    parts[h].append(lanes_of(prod[h, j, i : i + 1], 16).astype(BF) * mask)
        high = jnp.concatenate(parts[0], axis=0)
        low = jnp.concatenate(parts[1], axis=0).astype(F8)
        got = lax.dot_general(high, onehot, NT, preferred_element_type=F32)
        rest = lax.dot_general(low, onehot8, NT, preferred_element_type=F32)
        acc[g * n : (g + 1) * n, :] += got + rest


def assemble(read, flag, damp_ref, out_ref, stage, wide_ref):
    source = iota((640, 640), 0)
    place = iota((640, 640), 1) == 9 * (source % CAM) + source // CAM
    place = (place & (source < TILE)).astype(F32).astype(BF)
    lane = iota((144, PTS), 1)
    for u in range(4):
        base = (u // 2) * 128
        tiles = []
        for jj in range(5):
            even = read(2 * jj, base)
            if u % 2:
                even = pltpu.roll(even, 64, 1)
            if jj < 4:
                odd = read(2 * jj + 1, base)
                if u % 2 == 0:
                    odd = pltpu.roll(odd, 64, 1)
                even = jnp.where(lane < CAM, even, odd)
            tiles.append(even)
        full = jnp.concatenate(tiles, axis=1) * (1.0 / SCALE)
        high = full.astype(BF)
        wide_ref[144 * u : 144 * u + 144] = high
        wide_ref[TILE + 144 * u : TILE + 144 * u + 144] = (full - high.astype(F32)).astype(BF)
    got = jnp.dot(wide_ref[...], place, preferred_element_type=F32)
    got = got[:TILE] + got[TILE:]
    for u in range(4):
        for tile in range(5):
            for i in range(9):
                at = 144 * u + 16 * i
                piece = got[at : at + 16, 128 * tile : 128 * tile + 128]
                stage[pl.ds(TILE * tile + 144 * u + i, 16, stride=9), :] = piece
    for tile in range(5):
        wide = min(128, TILE - 128 * tile)
        block = stage[TILE * tile : TILE * tile + TILE, 0:wide]
        out_ref[0, :, 128 * tile : 128 * tile + wide] = block

    @pl.when(flag == 1)
    def _():
        same = iota((TILE, TILE), 0) == iota((TILE, TILE), 1)
        out_ref[0] += jnp.where(same, jnp.broadcast_to(damp_ref[...], (TILE, TILE)), 0.0)


def spread_kernel(e, flag_ref, damp_ref, *refs):
    if e:
        one, two, out_ref, token, prod, acc, stage, wide_ref = refs[0], refs[1], *refs[4:]
    else:
        in_ref, out_ref, one, prod, acc, stage, wide_ref = refs
    step = pl.program_id(0)

    @pl.when(step == 0)
    def _():
        acc[...] = jnp.zeros_like(acc)

    if e:
        add_products(1, one, two, prod, acc)
    else:
        lay(in_ref, one)
        add_products(0, one, None, prod, acc)

    @pl.when(step == pl.num_programs(0) - 1)
    def _():
        def read(j, base):
            return acc[144 * j : 144 * j + 144, base : base + 128]

        assemble(read, flag_ref[e], damp_ref, out_ref, stage, wide_ref)
        if e:
            token[...] = jnp.zeros_like(token)


def spread(e, flags, damp, args):
    steps = NDEV // SRC
    in_specs = [pl.BlockSpec(memory_space=pltpu.SMEM), whole(1, TILE)]
    tile_spec = pl.BlockSpec((1, TILE, TILE), lambda s: (e, 0, 0))
    tile_shape = jax.ShapeDtypeStruct((2, TILE, TILE), F32)
    if e:
        in_specs += [
            pl.BlockSpec((FIRST_ROWS, LANES), lambda s: (0, s)),
            pl.BlockSpec((SECOND_ROWS, LANES), lambda s: (0, s)),
            ANY,
            ANY,
        ]
        out_specs = [tile_spec, whole(8, 128)]
        out_shape = [tile_shape, jax.ShapeDtypeStruct((8, 128), F32)]
    else:
        in_specs.append(pl.BlockSpec((SRC, FIRST, PTS), lambda s: (s, 0, 0)))
        out_specs = [tile_spec, pl.BlockSpec((FIRST_ROWS, LANES), lambda s: (0, s))]
        out_shape = [tile_shape, jax.ShapeDtypeStruct((FIRST_ROWS, steps * LANES), F32)]
    return pl.pallas_call(
        functools.partial(spread_kernel, e),
        grid=(steps,),
        in_specs=in_specs,
        out_specs=out_specs,
        out_shape=out_shape,
        scratch_shapes=[
            pltpu.VMEM((2, 9, 16, LANES), F32),
            pltpu.VMEM((1296, 256), F32),
            pltpu.VMEM((5 * TILE, 128), F32),
            pltpu.VMEM((2 * TILE, 640), BF),
        ],
        input_output_aliases={4: 0} if e else {},
        name="spread",
        **settings(20, 44),
    )(flags, damp, *args)


def finish_kernel(in_ref, behind, step_ref, res_ref, dir_ref, both, image):
    step = pl.program_id(0)
    rows = in_ref.shape[0] // NCL
    lane = iota((8, 128), 1)
    flat = in_ref.reshape(NDEV // 2 * 16, 128)
    for k in range(rows):
        r = step * rows + k
        share = jnp.sum(in_ref[NCL * k : NCL * k + NCL], axis=0)
        image[pl.ds(r, 16, stride=8), :] = share
        for t in range(3):
            at = NCL * 16 * k + 9 + t
            even = flat[pl.ds(at, 8, stride=32), :]
            odd = flat[pl.ds(at + 16, 8, stride=32), :]
            both[3 * r + t] = jnp.where(lane < CAM, even, pltpu.roll(odd, CAM, 1))

    @pl.when(step == pl.num_programs(0) - 1)
    def _():
        def total(values):
            return jnp.sum(sum(values), keepdims=True)

        rhs = [both[i] for i in range(8)] + [both[16]]
        diag = [both[8 + i] for i in range(8)] + [both[17]]
        product = [image[8 * i : 8 * i + 8] for i in range(9)]
        start = [a / b for a, b in zip(rhs, diag)]
        rz = total([a * b for a, b in zip(rhs, start)])
        alpha = rz / total([a * b for a, b in zip(start, product)])
        residual = [a - alpha * b for a, b in zip(rhs, product)]
        second = [a / b for a, b in zip(residual, diag)]
        beta = total([a * b for a, b in zip(residual, second)]) / rz
        values = (
            [alpha * a for a in start],
            residual,
            [a + beta * b for a, b in zip(second, start)],
        )
        for r in range(9):
            at = 128 * r + lane
            camera = at // 9
            which = at - 9 * camera
            for value, ref in zip(values, (step_ref, res_ref, dir_ref)):
                row = jnp.take_along_axis(value[0], camera, axis=1)
                for i in range(1, 9):
                    row = jnp.where(which == i, jnp.take_along_axis(value[i], camera, axis=1), row)
                ref[pl.ds(r, 8, stride=9), :] = row


def finish(incoming, behind):
    return pl.pallas_call(
        finish_kernel,
        grid=(2,),
        in_specs=[pl.BlockSpec((NDEV // 2, 16, 128), lambda s: (s, 0, 0)), ANY],
        out_specs=[whole(72, 128)] * 3,
        out_shape=[jax.ShapeDtypeStruct((72, 128), F32)] * 3,
        scratch_shapes=[pltpu.VMEM((24, 8, 128), F32), pltpu.VMEM((128, 128), F32)],
        name="finish",
        **settings(3, 63),
    )(incoming, behind)


def shards(jac_cam, jac_pt, resid, point_damp, cam_damp, obs_cluster, obs_slot):
    my_row = lax.axis_index("row")
    my_col = lax.axis_index("col")
    flags = (2 * my_row + jnp.arange(2) == my_col).astype(jnp.int32)
    flags = jnp.concatenate([flags, my_row[None].astype(jnp.int32)])
    damp = cam_damp.reshape(CAM, 9).T
    zeros = jnp.zeros((8, CAM), F32)
    damp = jnp.concatenate([zeros, damp[0:8], zeros[0:1], damp[8:9], zeros[0:6]], axis=0)
    first, dense, found = pack_first(
        jac_cam.transpose(1, 0, 2), jac_pt.transpose(1, 0, 2), resid, point_damp, obs_cluster.T,
        obs_slot,
    )
    first = exchange(first.reshape(NDEV, FIRST, PTS))
    second = exchange(pack_second(dense, found).reshape(NDEV, SECOND // 4, 4, PTS))
    tiles, one = spread(0, flags, cam_damp, (first,))
    two, share = cg_part(flags, one, second, damp)
    shares = exchange(share)
    tiles, token = spread(1, flags, cam_damp, (one, two, tiles, share))
    step, residual, direction = finish(shares, token)
    return (tiles[:, None], step.reshape(-1), residual.reshape(-1), direction.reshape(-1))


def solution(mesh):
    placed = (
        P(None, None, AXES),
        P(None, None, AXES),
        P(None, None, AXES),
        P(None, AXES),
        P("col", None),
        P(AXES, None),
        P(None, AXES),
    )
    return jax.shard_map(
        shards,
        mesh=mesh,
        in_specs=placed,
        out_specs=(P("row", "col", None, None), P(), P(), P()),
        check_vma=False,
    )
```
